512 devices in a mesh: row: 32 (over z, x_lo), col: 16 (over x_hi, y, core).
Axes of the slice: x: 4 (x_hi: 2, x_lo: 2; x = x_hi * 2 + x_lo), y: 4, z: 16, core: 2. Of those that a mesh axis runs over, the one named last changes fastest.
Arguments:
- spectra: float32 [2, 2, 512, 10240], P(None, None, 'row', 'col'), may hold values from -6 to 6
Outputs:
- cross_spectra: float32 [2, 2, 10240, 10240], P(None, None, 'row', 'col')
The draws below stay inside these ranges and needn't reach their ends.
All inputs are finite; a program needn't handle non-finite values.
Results may differ from the reference program's by a relative error of at most 0.000094.
Values sent between devices are 32-bit elements; how exact they have to be, the bound alone decides.
A program may use at most 128 MiB of HBM per device.

```python
import jax
import jax.numpy as jnp
from jax import lax

C = 10240
F = 2
S = 512


def spiked(entries, rng, source, target, parts, factor):
    def block_of(axis_at):
        return (jnp.arange(entries.shape[axis_at]) // (entries.shape[axis_at] // parts)).reshape((-1,) + (1,) * (entries.ndim - 1 - axis_at))

    first = jax.random.permutation(rng, parts)[block_of(target)]
    second = (block_of(target) + parts // 2) % parts
    return jnp.where((block_of(source) == first) | (block_of(source) == second), factor * entries, entries)


def steps_of(stream_key, extent, cuts, smallest, largest):
    loudness, own = 1.0, jax.random.fold_in(stream_key, 6)
    for axis_at, blocks in cuts:
        heights = jnp.exp(jax.random.uniform(jax.random.fold_in(own, axis_at), (blocks,), jnp.float32, smallest / len(cuts), largest / len(cuts)))
        loudness = loudness * jnp.repeat(heights, extent[axis_at] // blocks).reshape([-1 if axis == axis_at else 1 for axis in range(len(extent))])
    return loudness


def noise_with(key, shape, scale, bound, shards, heavy, held_as=jnp.bfloat16):
    values = scale * jax.random.normal(key, shape, jnp.float32)
    if shards:
        values = values * steps_of(key, shape, shards, -0.22, 0.18)
    return jnp.clip(spiked(values, jax.random.fold_in(key, 3), *heavy), -bound, bound).astype(held_as)


def setup_inputs(seed: int = 0) -> dict:
    key_of = jax.random.split(jax.random.key(seed), 2)
    spectra = noise_with(key_of[0], (F, 2, S, C), 1.0, 6.0, ((2, 32), (3, 16)), (2, 3, 32, 2.75), jnp.float32)
    return {"spectra": spectra}


def contract(left_part, right_part):
    return lax.dot_general(left_part, right_part, (((0,), (0,)), ((), ())), precision=lax.Precision.HIGHEST, preferred_element_type=jnp.float32)


def per_bin(bin_spectra):
    real_part = bin_spectra[0]
    imag_part = bin_spectra[1]
    real_out = contract(real_part, real_part) + contract(imag_part, imag_part)
    imag_out = contract(imag_part, real_part) - contract(real_part, imag_part)
    segment_sums = jnp.stack([real_out, imag_out])
    return segment_sums / S


def reference(spectra):
    return lax.map(per_bin, spectra)
```

```python
import jax
import jax.numpy as jnp
from jax import lax
from jax.experimental import pallas as pl
from jax.experimental.pallas import tpu as pltpu
from jax.sharding import PartitionSpec as P

MESH = pl.DeviceIdType.MESH
CUT = 3
WIDE = 384


def kernel(x_ref, out_ref, col, row, lhs, rhs, own_sem, zs, zr, xs, xr, rr, ups, downs, mates, nears):
    r = lax.axis_index("row")
    c = lax.axis_index("col")
    z, xl = r // 2, r % 2
    xh, y, core = c // 8, (c // 2) % 4, c % 2
    src_xh, src_y, src_core = z // 8, (z // 2) % 4, z % 2
    dy = (y - src_y + 4) % 4
    home = xh == src_xh
    is_src = home & (dy == 0) & (core == src_core)
    is_src_mate = home & (dy == 0) & (core != src_core)
    is_near = jnp.logical_not(home) & (dy == 0)
    plain = jnp.logical_not(is_src | is_src_mate)
    lag = 1 + jnp.where(home, 0, 1) + jnp.where(dy == 0, 0, 1) + jnp.where(dy == 2, 1, 0)
    lag = lag + jnp.where(is_src_mate, 1, 0)

    zdev = [((r + 2) % 32, c), ((r + 30) % 32, c)]
    xdev = (r + 1 - 2 * xl, c)
    mate = (r, c + 1 - 2 * core)

    def ydev(step, k):
        return (r, xh * 8 + ((y + step + 4) % 4) * 2 + k)

    def ndev(k):
        return (r + 1 - 2 * xl, (1 - xh) * 8 + y * 2 + k)

    own = pltpu.make_async_copy(x_ref, col.at[0], own_sem)
    own.start()
    barrier = pltpu.get_barrier_semaphore()
    greet = [zdev[0], zdev[1], xdev, mate]
    greet += [ydev(s, k) for s in (1, -1) for k in (0, 1)] + [ndev(0), ndev(1)]
    for d in greet:
        pl.semaphore_signal(barrier, inc=1, device_id=d, device_id_type=MESH)
    own.wait()
    pl.semaphore_wait(barrier, len(greet))

    A, B = pl.ds(0, CUT), pl.ds(CUT, 8 - CUT)

    def remote(src, dst, ss, rs, dev):
        return pltpu.make_async_remote_copy(
            src_ref=src, dst_ref=dst, send_sem=ss, recv_sem=rs, device_id=dev, device_id_type=MESH
        )

    def zcopy(t, d, part):
        to = 4 * t - 2 + 2 * d
        fro = jnp.where(t == 1, 0, 4 * t - 6 + 2 * d)
        side, blocks = (1, A) if part == 2 else (0, (B, A)[part])
        return remote(
            col.at[fro + side, blocks], col.at[to + side, blocks], zs.at[d, t - 1, part], zr.at[d, t - 1, part], zdev[d]
        )

    def last_a():
        return remote(col.at[29, A], col.at[31, A], zs.at[1, 7, 2], zr.at[1, 7, 2], zdev[1])

    def last_b():
        return remote(col.at[29, B], col.at[31, B], zs.at[1, 7, 0], zr.at[1, 7, 0], zdev[1])

    def xown(part):
        blocks = (A, B)[part]
        return remote(col.at[0, blocks], col.at[1, blocks], xs.at[part, 0], xr.at[part, 0], xdev)

    def xcopy(t, d):
        slot = 4 * t - 2 + 2 * d
        return remote(col.at[slot, B], col.at[slot + 1, B], xs.at[d, t], xr.at[d, t], xdev)

    lanes_own = pl.ds(pl.multiple_of(256 * xl, 128), WIDE)
    lanes_far = pl.ds(pl.multiple_of(256 * (1 - xl), 128), WIDE)

    def pair(m):
        return pl.ds(2 * m, 2)

    def rows_copy(m, src, sems, dev):
        return remote(src, row.at[pair(m)], sems.at[m], rr.at[m], dev)

    def rows_wait(m):
        pltpu.make_async_copy(row.at[pair(m)], row.at[pair(m)], rr.at[m]).wait()

    def source_sends(m):
        src = col.at[pair(m), :, :, lanes_own]
        k = m % 2
        far = [
            remote(col.at[2 * m + s, :, :, lanes_far], row.at[2 * m + 1 - s], nears.at[m], rr.at[m], ndev(k))
            for s in (0, 1)
        ]
        return far, [
            rows_copy(m, src, ups, ydev(1, k)),
            rows_copy(m, src, downs, ydev(-1, k)),
            rows_copy(m, src, mates, mate),
        ]

    def source_start(m):
        far, rest = source_sends(m)
        for cp in far + rest:
            cp.start()
        pltpu.make_async_copy(col.at[pair(m), :, :, lanes_own], row.at[pair(m)], rr.at[m]).start()

    def relay_up(m):
        return is_near | ((dy == 1) & ((m // 2) % 2 == 0))

    def relay_down(m):
        return is_near | ((dy == 3) & ((m // 2) % 2 == 1))

    def relay(m):
        src = row.at[pair(m)]
        rows_wait(m)

        @pl.when(relay_up(m))
        def _():
            rows_copy(m, src, ups, ydev(1, core)).start()

        @pl.when(relay_down(m))
        def _():
            rows_copy(m, src, downs, ydev(-1, core)).start()

        rows_copy(m, src, mates, mate).start()

    def split(v):
        hi = v.astype(jnp.bfloat16)
        return hi, (v - hi.astype(jnp.float32)).astype(jnp.bfloat16)

    def compute(q, f):
        slots, blocks = pl.ds(8 * q, 8), pl.ds(4 * f, 4)
        w = row[slots, blocks].reshape(256, WIDE).T
        lhs[0], lhs[1] = split(w)
        v = col[slots, blocks].reshape(8, 2, 16, 640)
        for part, value in enumerate(split(v)):
            rhs[part, :, :640] = value.reshape(256, 640)
            swapped = jnp.concatenate([-value[:, 1:2], value[:, 0:1]], axis=1)
            rhs[part, :, 640:] = swapped.reshape(256, 640)
        rows = pl.ds(pl.multiple_of(64 * xl, 64), 320)
        l_hi, l_lo = lhs[0, rows], lhs[1, rows]
        for n in range(5):
            lanes = slice(256 * n, 256 * n + 256)
            r_hi, r_lo = rhs[0, :, lanes], rhs[1, :, lanes]
            total = jnp.dot(l_hi, r_hi, preferred_element_type=jnp.float32)
            total += jnp.dot(l_lo, r_hi, preferred_element_type=jnp.float32)
            total += jnp.dot(l_hi, r_lo, preferred_element_type=jnp.float32)
            for half in (0, 1):
                at = 256 * n + 128 * half
                p, j = at // 640, at % 640
                out_ref[f, p, :, j : j + 128] += total[:, 128 * half : 128 * half + 128]

    for d in (0, 1):
        zcopy(1, d, 0).start()
        zcopy(1, d, 1).start()
    xown(0).start()
    xown(1).start()
    out_ref[...] = jnp.zeros_like(out_ref)
    xown(0).wait_recv()
    for d in (0, 1):
        zcopy(1, d, 2).start()

    def step(k, carry):
        @pl.when(k <= 7)
        def _():
            for part in (0, 1, 2):
                for d in (0, 1):
                    zcopy(k, d, part).wait_recv()

                    @pl.when(k < 7)
                    def _():
                        zcopy(k + 1, d, part).start()

                    if part == 0:
                        xcopy(k, d).start()
                    if part < 2 and d == 0:

                        @pl.when(k == 7)
                        def _():
                            zcopy(k + 1, d, part).start()

                    if part == 2 and d == 1:

                        @pl.when(k == 7)
                        def _():
                            last_a().start()

        @pl.when(k == 1)
        def _():
            xown(1).wait_recv()

        @pl.when((k >= 2) & (k <= 8))
        def _():
            for d in (0, 1):
                xcopy(k - 1, d).wait_recv()

        @pl.when(k == 8)
        def _():
            last_b().start()
            zcopy(k, 0, 0).wait_recv()
            zcopy(k, 0, 1).wait_recv()
            last_a().wait_recv()

        @pl.when(k == 9)
        def _():
            last_b().wait_recv()

        for m in (2 * k - 3, 2 * k - 2):

            @pl.when(is_src & (m >= 0) & (m <= 15))
            def _():
                source_start(m)

        m = 2 * (k - lag) - core

        @pl.when(plain & (m >= 0) & (m <= 15))
        def _():
            relay(m)

        at = k - lag - 3
        q, f = at // 2, at % 2

        @pl.when((at >= 0) & (at <= 7))
        def _():
            @pl.when(f == 0)
            def _():
                for i in range(4):

                    @pl.when(jnp.logical_not(plain) | (i % 2 != core))
                    def _():
                        rows_wait(4 * q + i)

            compute(q, f)

        return carry

    lax.fori_loop(1, 16, step, 0)

    def zdone(t, carry):
        for d in (0, 1):
            for part in (0, 1, 2):
                zcopy(t, d, part).wait_send()
            xcopy(t, d).wait_send()
        return carry

    lax.fori_loop(1, 8, zdone, 0)
    zcopy(8, 0, 0).wait_send()
    zcopy(8, 0, 1).wait_send()
    last_a().wait_send()
    last_b().wait_send()
    xown(0).wait_send()
    xown(1).wait_send()

    def rdone(m, carry):
        mine = plain & (m % 2 == core)
        src = row.at[pair(m)]

        @pl.when(is_src)
        def _():
            rows_copy(m, src, nears, mate).wait_send()

        @pl.when(is_src | (mine & relay_up(m)))
        def _():
            rows_copy(m, src, ups, mate).wait_send()

        @pl.when(is_src | (mine & relay_down(m)))
        def _():
            rows_copy(m, src, downs, mate).wait_send()

        @pl.when(is_src | mine)
        def _():
            rows_copy(m, src, mates, mate).wait_send()

        return carry

    lax.fori_loop(0, 16, rdone, 0)


def per_device(spectra):
    shard = spectra.reshape(8, 8, 640)
    dma = pltpu.SemaphoreType.DMA
    sums = pl.pallas_call(
        kernel,
        out_shape=jax.ShapeDtypeStruct((2, 2, 320, 640), jnp.float32),
        in_specs=[pl.BlockSpec(memory_space=pl.ANY)],
        out_specs=pl.BlockSpec(memory_space=pltpu.VMEM),
        scratch_shapes=[
            pltpu.VMEM((32, 8, 8, 640), jnp.float32),
            pltpu.VMEM((32, 8, 8, WIDE), jnp.float32),
            pltpu.VMEM((2, WIDE, 256), jnp.bfloat16),
            pltpu.VMEM((2, 256, 1280), jnp.bfloat16),
            dma,
            dma((2, 8, 3)),
            dma((2, 8, 3)),
            dma((2, 8)),
            dma((2, 8)),
            dma((16,)),
            dma((16,)),
            dma((16,)),
            dma((16,)),
            dma((16,)),
        ],
        compiler_params=pltpu.CompilerParams(
            collective_id=0, has_side_effects=True, vmem_limit_bytes=28 * 2**20
        ),
        name="gather_and_multiply",
    )(shard)
    return sums * (1.0 / 512.0)


def solution(mesh):
    return jax.shard_map(
        per_device,
        mesh=mesh,
        in_specs=(P(None, None, "row", "col"),),
        out_specs=P(None, None, "row", "col"),
        check_vma=False,
    )
```

```python
import jax
import jax.numpy as jnp
from jax import lax
from jax.experimental import pallas as pl
from jax.experimental.pallas import tpu as pltpu
from jax.sharding import PartitionSpec as P

MESH = pl.DeviceIdType.MESH
CUT = 3
HALF = 10
TILES = 2 * HALF


def kernel(x_ref, out_ref, col, row, far, lhs, rhs, own_sem, zs, zr, xs, xr, rr, ups, downs, mates, nears):
    r = lax.axis_index("row")
    c = lax.axis_index("col")
    z, xl = r // 2, r % 2
    xh, y, core = c // 8, (c // 2) % 4, c % 2
    src_xh, src_y, src_core = z // 8, (z // 2) % 4, z % 2
    dy = (y - src_y + 4) % 4
    home = xh == src_xh
    is_src = home & (dy == 0) & (core == src_core)
    is_src_mate = home & (dy == 0) & (core != src_core)
    is_near = jnp.logical_not(home) & (dy == 0)
    plain = jnp.logical_not(is_src | is_src_mate)
    hops = jnp.where(home, 0, 1) + jnp.where(dy == 0, 0, 1) + jnp.where(dy == 2, 1, 0)
    lag = jnp.maximum(hops - 1, 0)
    turns = (hops + 1 + jnp.where(hops == 3, 1, 0), 2 * hops + jnp.where(hops == 3, 0, 1))
    flip = jnp.where(home, 0, 1)

    zdev = [((r + 2) % 32, c), ((r + 30) % 32, c)]
    xdev = (r + 1 - 2 * xl, c)
    mate = (r, c + 1 - 2 * core)

    def ydev(step, k):
        return (r, xh * 8 + ((y + step + 4) % 4) * 2 + k)

    def ndev(k):
        return (r + 1 - 2 * xl, (1 - xh) * 8 + y * 2 + k)

    own = pltpu.make_async_copy(x_ref, col.at[0], own_sem)
    own.start()
    barrier = pltpu.get_barrier_semaphore()
    greet = [zdev[0], zdev[1], xdev, mate]
    greet += [ydev(s, k) for s in (1, -1) for k in (0, 1)] + [ndev(0), ndev(1)]
    for d in greet:
        pl.semaphore_signal(barrier, inc=1, device_id=d, device_id_type=MESH)
    own.wait()
    pl.semaphore_wait(barrier, len(greet))

    A, B = pl.ds(0, CUT), pl.ds(CUT, 8 - CUT)

    def remote(src, dst, ss, rs, dev):
        return pltpu.make_async_remote_copy(
            src_ref=src, dst_ref=dst, send_sem=ss, recv_sem=rs, device_id=dev, device_id_type=MESH
        )

    def zcopy(t, d, part):
        to = 4 * t - 2 + 2 * d
        fro = jnp.where(t == 1, 0, 4 * t - 6 + 2 * d)
        side, blocks = (1, A) if part == 2 else (0, (B, A)[part])
        return remote(
            col.at[fro + side, blocks], col.at[to + side, blocks], zs.at[d, t - 1, part], zr.at[d, t - 1, part], zdev[d]
        )

    def last_a():
        return remote(col.at[29, A], col.at[31, A], zs.at[1, 7, 2], zr.at[1, 7, 2], zdev[1])

    def last_b():
        return remote(col.at[29, B], col.at[31, B], zs.at[1, 7, 0], zr.at[1, 7, 0], zdev[1])

    def xown(part):
        blocks = (A, B)[part]
        return remote(col.at[0, blocks], col.at[1, blocks], xs.at[part, 0], xr.at[part, 0], xdev)

    def xcopy(t, d):
        slot = 4 * t - 2 + 2 * d
        return remote(col.at[slot, B], col.at[slot + 1, B], xs.at[d, t], xr.at[d, t], xdev)

    def half(f):
        return pl.ds(HALF * f, HALF)

    def rows_copy(s, f, src, sems, dev, to=None):
        to = s if to is None else to
        return remote(src.at[s, half(f)], row.at[to, half(f)], sems.at[s], rr.at[2 * to + f], dev)

    def rows_wait(s, f):
        pltpu.make_async_copy(row.at[s, half(f)], row.at[s, half(f)], rr.at[2 * s + f]).wait()

    def sent(s, sems):
        remote(row.at[s], row.at[s], sems.at[s], rr.at[2 * s], mate).wait_send()

    def other(s):
        return s + 1 - 2 * (s % 2)

    def pack(s):
        low = lax.broadcasted_iota(jnp.int32, (32, 128), 1) < 64
        mid = col[s, :, :, 256:384].reshape(2, 2, 2, 8, 128)
        re, im = mid[:, 0].reshape(32, 128), mid[:, 1].reshape(32, 128)
        first = jnp.where(low, re, pltpu.roll(im, 64, 1))
        second = jnp.where(low, pltpu.roll(re, 64, 1), im)
        for buf, side in ((row, xl), (far, 1 - xl)):
            packed = jnp.where(side == 0, first, second).reshape(2, 2, 8, 128)
            for f in (0, 1):
                for a in (0, 1):
                    lanes = pl.ds(pl.multiple_of(384 * side + 128 * a, 128), 128)
                    at = HALF * f + 4 * a
                    buf[s, at : at + 4] = col[s, 4 * f : 4 * f + 4, :, lanes]
                buf[s, HALF * f + 8 : HALF * f + 10] = packed[f]

    def source_start(s):
        pack(s)
        k = (s // 2) % 2
        for f in (0, 1):
            rows_copy(s, f, far, nears, ndev(k), other(s)).start()
            rows_copy(s, f, row, ups, ydev(1, k)).start()
            rows_copy(s, f, row, downs, ydev(-1, k)).start()
            rows_copy(s, f, row, mates, mate).start()

    def relay_up(kind):
        return is_near | ((dy == 1) & (kind == 0))

    def relay_down(kind):
        return is_near | ((dy == 3) & (kind == 1))

    def relay(s, kind):
        for f in (0, 1):
            rows_wait(s, f)

            @pl.when(relay_up(kind))
            def _():
                rows_copy(s, f, row, ups, ydev(1, core)).start()

            @pl.when(relay_down(kind))
            def _():
                rows_copy(s, f, row, downs, ydev(-1, core)).start()

            rows_copy(s, f, row, mates, mate).start()

    def split(v):
        hi = v.astype(jnp.bfloat16)
        return hi, (v - hi.astype(jnp.float32)).astype(jnp.bfloat16)

    def compute(q, f):
        slots = pl.ds(8 * q, 8)
        for p in (0, 1):
            depth = slice(128 * p, 128 * p + 128)
            for a in (0, 1):
                w = row[slots, pl.ds(HALF * f + 4 * a + 2 * p, 2)].reshape(128, 128).T
                at = pl.ds(pl.multiple_of(64 * xl + 128 * a, 64), 128)
                lhs[0, at, depth], lhs[1, at, depth] = split(w)
        w = row[slots, pl.ds(HALF * f + 8, 2)].reshape(128, 128).T
        at = pl.ds(pl.multiple_of(256 * (1 - xl), 64), 64)
        for part, value in enumerate(split(w)):
            lhs[part, at, :128], lhs[part, at, 128:] = value[:64], value[64:]
        for part, (re, im) in enumerate(zip(*[split(col[slots, pl.ds(4 * f + 2 * p, 2)].reshape(128, 640)) for p in (0, 1)])):
            rhs[part, :128, :640], rhs[part, 128:, :640] = re, im
            rhs[part, :128, 640:], rhs[part, 128:, 640:] = -im, re
        l_hi, l_lo = lhs[0], lhs[1]
        for n in range(5):
            lanes = slice(256 * n, 256 * n + 256)
            r_hi, r_lo = rhs[0, :, lanes], rhs[1, :, lanes]
            total = jnp.dot(l_hi, r_hi, preferred_element_type=jnp.float32)
            total += jnp.dot(l_lo, r_hi, preferred_element_type=jnp.float32)
            total += jnp.dot(l_hi, r_lo, preferred_element_type=jnp.float32)
            for half in (0, 1):
                at = 256 * n + 128 * half
                p, j = at // 640, at % 640
                out_ref[f, p, :, j : j + 128] += total[:, 128 * half : 128 * half + 128]

    for d in (0, 1):
        zcopy(1, d, 0).start()
        zcopy(1, d, 1).start()
    xown(0).start()
    xown(1).start()
    out_ref[...] = jnp.zeros_like(out_ref)
    xown(0).wait_recv()
    for d in (0, 1):
        zcopy(1, d, 2).start()

    def source_sends(at, kind):
        for d in (0, 1):
            s = 4 * at - 2 + 2 * d + kind

            @pl.when(is_src & (s >= 0) & (s <= 31))
            def _():
                source_start(s)

    def step(k, carry):
        ring = (k >= 1) & (k <= 7)

        def arrive(part):
            for d in (1, 0):
                zcopy(k, d, part).wait_recv()

                @pl.when(k < 7)
                def _():
                    zcopy(k + 1, d, part).start()

                if part == 0:
                    xcopy(k, d).start()
                if part < 2 and d == 0:

                    @pl.when(k == 7)
                    def _():
                        zcopy(k + 1, d, part).start()

                if part == 2 and d == 1:

                    @pl.when(k == 7)
                    def _():
                        last_a().start()

        def relays(turn):
            for kind in (1, 0):
                t = turn - turns[kind]
                s = 2 * t - 2 * core + (flip if kind == 0 else 1 - flip)

                @pl.when(plain & (t % 2 == 0) & (s >= 0) & (s <= 31))
                def _():
                    relay(s, kind)

        @pl.when(ring)
        def _():
            arrive(0)

        @pl.when(k == 1)
        def _():
            xown(1).wait_recv()

        @pl.when((k >= 2) & (k <= 8))
        def _():
            xcopy(k - 1, 1).wait_recv()

            @pl.when(k == 8)
            def _():
                last_b().start()

            xcopy(k - 1, 0).wait_recv()

        @pl.when(k == 9)
        def _():
            last_a().wait_recv()
            last_b().wait_recv()

        source_sends(k - 1, 1)
        relays(2 * k)

        @pl.when(ring)
        def _():
            arrive(1)

        @pl.when(k == 8)
        def _():
            zcopy(k, 0, 0).wait_recv()
            zcopy(k, 0, 1).wait_recv()

        source_sends(k, 0)

        at = k - lag - 4
        q, f = at // 2, at % 2

        @pl.when((at >= 0) & (at <= 7))
        def _():
            for i in range(8):

                @pl.when(is_src_mate | (plain & ((i // 2) % 2 != core)))
                def _():
                    rows_wait(8 * q + i, f)

            compute(q, f)

        @pl.when(ring)
        def _():
            arrive(2)

        relays(2 * k + 1)
        return carry

    lax.fori_loop(0, 14, step, 0)

    def zdone(t, carry):
        for d in (0, 1):
            for part in (0, 1, 2):
                zcopy(t, d, part).wait_send()
            xcopy(t, d).wait_send()
        return carry

    lax.fori_loop(1, 8, zdone, 0)
    zcopy(8, 0, 0).wait_send()
    zcopy(8, 0, 1).wait_send()
    last_a().wait_send()
    last_b().wait_send()
    xown(0).wait_send()
    xown(1).wait_send()

    def rdone(s, carry):
        mine = plain & ((s // 2) % 2 == core)
        kind = (s + flip) % 2

        @pl.when(is_src)
        def _():
            sent(s, nears)

        @pl.when(is_src | (mine & relay_up(kind)))
        def _():
            sent(s, ups)

        @pl.when(is_src | (mine & relay_down(kind)))
        def _():
            sent(s, downs)

        @pl.when(is_src | mine)
        def _():
            sent(s, mates)

        return carry

    lax.fori_loop(0, 32, rdone, 0)


def per_device(spectra):
    shard = spectra.reshape(8, 8, 640)
    dma = pltpu.SemaphoreType.DMA
    sums = pl.pallas_call(
        kernel,
        out_shape=jax.ShapeDtypeStruct((2, 2, 320, 640), jnp.float32),
        in_specs=[pl.BlockSpec(memory_space=pltpu.HBM)],
        out_specs=pl.BlockSpec(memory_space=pltpu.VMEM),
        scratch_shapes=[
            pltpu.VMEM((32, 8, 8, 640), jnp.float32),
            pltpu.VMEM((32, TILES, 8, 128), jnp.float32),
            pltpu.VMEM((32, TILES, 8, 128), jnp.float32),
            pltpu.VMEM((2, 320, 256), jnp.bfloat16),
            pltpu.VMEM((2, 256, 1280), jnp.bfloat16),
            dma,
            dma((2, 8, 3)),
            dma((2, 8, 3)),
            dma((2, 8)),
            dma((2, 8)),
            dma((64,)),
            dma((32,)),
            dma((32,)),
            dma((32,)),
            dma((32,)),
        ],
        compiler_params=pltpu.CompilerParams(
            collective_id=0, has_side_effects=True, vmem_limit_bytes=28 * 2**20
        ),
        name="gather_and_multiply",
    )(pltpu.with_memory_space_constraint(shard, pltpu.HBM))
    return sums * (1.0 / 512.0)


def solution(mesh):
    return jax.shard_map(
        per_device,
        mesh=mesh,
        in_specs=(P(None, None, "row", "col"),),
        out_specs=P(None, None, "row", "col"),
        check_vma=False,
    )
```

```python
import jax
import jax.numpy as jnp
from jax import lax
from jax.experimental import pallas as pl
from jax.experimental.pallas import tpu as pltpu
from jax.sharding import PartitionSpec as P

MESH = pl.DeviceIdType.MESH
CUT = 3
HALF = 10
PAD = 2
TILES = 2 * HALF


def kernel(x_ref, out_ref, col, row, far, lhs, rhs, own_sem, zs, zr, xs, xr, rr, rs):
    ups, downs, mates, nears = 0, 1, 2, 3
    r = lax.axis_index("row")
    c = lax.axis_index("col")
    z, xl = r // 2, r % 2
    xh, y, core = c // 8, (c // 2) % 4, c % 2
    src_xh, src_y, src_core = z // 8, (z // 2) % 4, z % 2
    dy = (y - src_y + 4) % 4
    home = xh == src_xh
    is_src = home & (dy == 0) & (core == src_core)
    is_src_mate = home & (dy == 0) & (core != src_core)
    is_near = jnp.logical_not(home) & (dy == 0)
    plain = jnp.logical_not(is_src | is_src_mate)
    hops = jnp.where(home, 0, 1) + jnp.where(dy == 0, 0, 1) + jnp.where(dy == 2, 1, 0)
    lag = jnp.where(hops >= 2, 1, 0)
    turns = (hops + 1 + jnp.where(hops == 3, 1, 0), 2 * hops + jnp.where(hops == 3, 0, 1))
    flip = jnp.where(home, 0, 1)

    zdev = [((r + 2) % 32, c), ((r + 30) % 32, c)]
    xdev = (r + 1 - 2 * xl, c)
    mate = (r, c + 1 - 2 * core)

    def ydev(step, k):
        return (r, xh * 8 + ((y + step + 4) % 4) * 2 + k)

    def ndev(k):
        return (r + 1 - 2 * xl, (1 - xh) * 8 + y * 2 + k)

    def blk(s, blocks):
        return pl.ds(8 * (s + PAD) + blocks.start, blocks.stop - blocks.start)

    own = pltpu.make_async_copy(x_ref, col.at[blk(0, slice(0, 8))], own_sem)
    own.start()
    barrier = pltpu.get_barrier_semaphore()
    greet = [zdev[0], zdev[1], xdev, mate]
    greet += [ydev(s, k) for s in (1, -1) for k in (0, 1)] + [ndev(0), ndev(1)]
    for d in greet:
        pl.semaphore_signal(barrier, inc=1, device_id=d, device_id_type=MESH)
    own.wait()
    pl.semaphore_wait(barrier, len(greet))

    A, B = slice(0, CUT), slice(CUT, 8)

    def remote(src, dst, ss, rs, dev):
        return pltpu.make_async_remote_copy(
            src_ref=src, dst_ref=dst, send_sem=ss, recv_sem=rs, device_id=dev, device_id_type=MESH
        )

    def zcopy(t, d, part):
        to = 4 * t - 2 + 2 * d
        fro = jnp.where(t == 1, 0, 4 * t - 6 + 2 * d)
        side, blocks = (1, A) if part == 2 else (0, (B, A)[part])
        return remote(
            col.at[blk(fro + side, blocks)], col.at[blk(to + side, blocks)], zs.at[d], zr.at[d, t - 1, part], zdev[d]
        )

    def last_a():
        return remote(col.at[blk(29, A)], col.at[blk(31, A)], zs.at[1], zr.at[1, 7, 2], zdev[1])

    def last_b():
        return remote(col.at[blk(29, B)], col.at[blk(31, B)], zs.at[1], zr.at[1, 7, 0], zdev[1])

    def xown(part):
        blocks = (A, B)[part]
        return remote(col.at[blk(0, blocks)], col.at[blk(1, blocks)], xs, xr.at[part, 0], xdev)

    def xcopy(t, d):
        slot = 4 * t - 2 + 2 * d
        return remote(col.at[blk(slot, B)], col.at[blk(slot + 1, B)], xs, xr.at[d, t], xdev)

    def half(f):
        return pl.ds(HALF * f, HALF)

    def rows_copy(s, f, src, way, dev, to=None):
        to = s if to is None else to
        return remote(src.at[s + PAD, half(f)], row.at[to + PAD, half(f)], rs.at[way], rr.at[2 * to + f], dev)

    def rows_wait(s, f):
        ref = row.at[s + PAD, half(f)]
        pltpu.make_async_copy(ref, ref, rr.at[2 * s + f]).wait()

    def sent(shards, way):
        ref = row.at[pl.ds(0, shards)]
        remote(ref, ref, rs.at[way], rr.at[0], mate).wait_send()

    def other(s):
        return s + 1 - 2 * (s % 2)

    def pack(s):
        low = lax.broadcasted_iota(jnp.int32, (32, 128), 1) < 64
        shard = pl.ds(8 * (s + PAD), 8)
        mid = col[shard, :, 256:384].reshape(2, 2, 2, 8, 128)
        re, im = mid[:, 0].reshape(32, 128), mid[:, 1].reshape(32, 128)
        first = jnp.where(low, re, pltpu.roll(im, 64, 1))
        second = jnp.where(low, pltpu.roll(re, 64, 1), im)
        for buf, side in ((row, xl), (far, 1 - xl)):
            packed = jnp.where(side == 0, first, second).reshape(2, 2, 8, 128)
            for f in (0, 1):
                for a in (0, 1):
                    lanes = pl.ds(pl.multiple_of(384 * side + 128 * a, 128), 128)
                    at = HALF * f + 4 * a
                    buf[s + PAD, at : at + 4] = col[pl.ds(8 * (s + PAD) + 4 * f, 4), :, lanes]
                buf[s + PAD, HALF * f + 8 : HALF * f + 10] = packed[f]

    def source_start(s):
        pack(s)
        k = (s // 2) % 2
        for f in (0, 1):
            rows_copy(s, f, far, nears, ndev(k), other(s)).start()
            rows_copy(s, f, row, ups, ydev(1, k)).start()
            rows_copy(s, f, row, downs, ydev(-1, k)).start()
            rows_copy(s, f, row, mates, mate).start()

    def relay_up(kind):
        return is_near | ((dy == 1) & (kind == 0))

    def relay_down(kind):
        return is_near | ((dy == 3) & (kind == 1))

    def relay(s, kind):
        for f in (0, 1):
            rows_wait(s, f)

            @pl.when(relay_up(kind))
            def _():
                rows_copy(s, f, row, ups, ydev(1, core)).start()

            @pl.when(relay_down(kind))
            def _():
                rows_copy(s, f, row, downs, ydev(-1, core)).start()

            rows_copy(s, f, row, mates, mate).start()

    def split(v):
        hi = v.astype(jnp.bfloat16)
        return hi, (v - hi.astype(jnp.float32)).astype(jnp.bfloat16)

    def add(f, n, total):
        for side in (0, 1):
            at = 256 * n + 128 * side
            p, j = at // 640, at % 640
            out_ref[f, p, :, j : j + 128] += total[:, 128 * side : 128 * side + 128]

    def rhs_store(part, at, re, im):
        n = re.shape[0]
        rhs[part, at : at + n, :640], rhs[part, at + n : at + 2 * n, :640] = re, im
        rhs[part, at : at + n, 640:], rhs[part, at + n : at + 2 * n, 640:] = -im, re

    def compute(q, f):
        slots = pl.ds(8 * q, 8)
        for p in (0, 1):
            depth = slice(128 * p, 128 * p + 128)
            for a in (0, 1):
                w = row[slots, pl.ds(HALF * f + 4 * a + 2 * p, 2)].reshape(128, 128).T
                at = pl.ds(pl.multiple_of(64 * xl + 128 * a, 64), 128)
                lhs[0, at, depth], lhs[1, at, depth] = split(w)
        w = row[slots, pl.ds(HALF * f + 8, 2)].reshape(128, 128).T
        at = pl.ds(pl.multiple_of(256 * (1 - xl), 64), 64)
        for part, value in enumerate(split(w)):
            lhs[part, at, :128], lhs[part, at, 128:] = value[:64], value[64:]
        col4 = col.reshape(32 + PAD, 8, 8, 640)
        (re_hi, re_lo), (im_hi, im_lo) = [
            split(col4[slots, pl.ds(4 * f + 2 * p, 2)].reshape(128, 640)) for p in (0, 1)
        ]
        rhs_store(0, 0, re_hi, im_hi)
        rhs_store(1, 0, re_lo, im_lo)
        l_hi, l_lo = lhs[0], lhs[1]
        for n in range(5):
            lanes = slice(256 * n, 256 * n + 256)
            r_hi, r_lo = rhs[0, :, lanes], rhs[1, :, lanes]
            total = jnp.dot(l_hi, r_hi, preferred_element_type=jnp.float32)
            total += jnp.dot(l_lo, r_hi, preferred_element_type=jnp.float32)
            total += jnp.dot(l_hi, r_lo, preferred_element_type=jnp.float32)
            add(f, n, total)

    def compute_last(f):
        slots = slice(30 + PAD, 32 + PAD)

        def stacked(w):
            hi = w.astype(jnp.bfloat16).astype(jnp.float32)
            return jnp.concatenate([hi, w - hi, hi, jnp.zeros_like(w)], axis=0).T.astype(jnp.bfloat16)

        for a in (0, 1):
            w = [row[slots, HALF * f + 4 * a + 2 * p : HALF * f + 4 * a + 2 * p + 2].reshape(32, 128) for p in (0, 1)]
            lhs[0, pl.ds(pl.multiple_of(64 * xl + 128 * a, 64), 128)] = stacked(jnp.concatenate(w, axis=0))
        w = row[slots, HALF * f + 8 : HALF * f + 10].reshape(32, 128)
        w = stacked(jnp.concatenate([w, pltpu.roll(w, 64, 1)], axis=0))
        lhs[0, pl.ds(pl.multiple_of(256 * (1 - xl), 64), 64)] = w[:64]
        col4 = col.reshape(32 + PAD, 8, 8, 640)
        (re_hi, re_lo), (im_hi, im_lo) = [
            split(col4[slots, 4 * f + 2 * p : 4 * f + 2 * p + 2].reshape(32, 640)) for p in (0, 1)
        ]
        rhs_store(0, 0, re_hi, im_hi)
        rhs_store(0, 64, re_hi, im_hi)
        rhs_store(0, 128, re_lo, im_lo)
        rhs[0, 192:] = jnp.zeros((64, 1280), jnp.bfloat16)
        left = lhs[0]
        for n in range(5):
            add(f, n, jnp.dot(left, rhs[0, :, 256 * n : 256 * n + 256], preferred_element_type=jnp.float32))

    for d in (0, 1):
        zcopy(1, d, 0).start()
        zcopy(1, d, 1).start()
    xown(0).start()
    xown(1).start()
    out_ref[...] = jnp.zeros_like(out_ref)
    col[: 8 * PAD] = jnp.zeros((8 * PAD, 8, 640), jnp.float32)
    row[:PAD] = jnp.zeros((PAD, TILES, 8, 128), jnp.float32)
    xown(0).wait_recv()
    for d in (0, 1):
        zcopy(1, d, 2).start()

    def source_sends(at, kind):
        for d in (0, 1):
            s = 4 * at - 2 + 2 * d + kind

            @pl.when(is_src & (s >= 0) & (s <= 31))
            def _():
                source_start(s)

    def others_wait(s, f):
        @pl.when((s >= 0) & (is_src_mate | (plain & ((s // 2) % 2 != core))))
        def _():
            rows_wait(s, f)

    def waited(at):
        q, f = at // 2, at % 2
        for i in range(8):
            others_wait(8 * q + i - PAD, f)
        compute(q, f)

    def step(k, carry):
        ring = (k >= 1) & (k <= 7)

        def arrive(part):
            for d in (1, 0):
                zcopy(k, d, part).wait_recv()

                @pl.when(k < 7)
                def _():
                    zcopy(k + 1, d, part).start()

                if part == 0:
                    xcopy(k, d).start()
                if part < 2 and d == 0:

                    @pl.when(k == 7)
                    def _():
                        zcopy(k + 1, d, part).start()

                if part == 2 and d == 1:

                    @pl.when(k == 7)
                    def _():
                        last_a().start()

        def relays(turn):
            for kind in (1, 0):
                t = turn - turns[kind]
                s = 2 * t - 2 * core + (flip if kind == 0 else 1 - flip)

                @pl.when(plain & (t % 2 == 0) & (s >= 0) & (s <= 31))
                def _():
                    relay(s, kind)

        @pl.when(ring)
        def _():
            arrive(0)

        @pl.when(k == 1)
        def _():
            xown(1).wait_recv()

        @pl.when((k >= 2) & (k <= 8))
        def _():
            xcopy(k - 1, 1).wait_recv()

            @pl.when(k == 8)
            def _():
                last_b().start()

            xcopy(k - 1, 0).wait_recv()

        @pl.when(k == 9)
        def _():
            last_a().wait_recv()
            last_b().wait_recv()

        source_sends(k - 1, 1)
        relays(2 * k)

        @pl.when(ring)
        def _():
            arrive(1)

        @pl.when(k == 8)
        def _():
            zcopy(k, 0, 0).wait_recv()
            zcopy(k, 0, 1).wait_recv()

        source_sends(k, 0)

        at = k - 3 - lag

        @pl.when((k <= 7) & (at >= 0))
        def _():
            waited(at)

        @pl.when(ring)
        def _():
            arrive(2)

        relays(2 * k + 1)
        at = jnp.where(hops == 3, k - 4, k - jnp.where(k <= 8, 2, 3) - lag)
        early = (k >= 7) & (k <= 8) & (at <= 5)
        late = (k >= 9) & (at >= jnp.where(hops == 3, 5, 6)) & (at <= 7)

        @pl.when(jnp.where(hops == 3, k >= 8, early | late))
        def _():
            waited(at)

        return carry

    lax.fori_loop(0, 12, step, 0)
    for f in (0, 1):
        for s in (30, 31):
            others_wait(s, f)
        compute_last(f)

    for d in (0, 1):
        ref = col.at[pl.ds(0, 7 * (8 + CUT) + 8)]
        remote(ref, ref, zs.at[d], zr.at[0, 0, 0], mate).wait_send()
    ref = col.at[pl.ds(0, 8 + 14 * (8 - CUT))]
    remote(ref, ref, xs, zr.at[0, 0, 0], mate).wait_send()

    @pl.when(is_src)
    def _():
        for way in (ups, downs, mates, nears):
            sent(32, way)

    @pl.when(is_near)
    def _():
        sent(16, ups)
        sent(16, downs)

    @pl.when(dy == 1)
    def _():
        sent(8, ups)

    @pl.when(dy == 3)
    def _():
        sent(8, downs)

    @pl.when(plain)
    def _():
        sent(16, mates)


def per_device(spectra):
    shard = spectra.reshape(8, 8, 640)
    dma = pltpu.SemaphoreType.DMA
    sums = pl.pallas_call(
        kernel,
        out_shape=jax.ShapeDtypeStruct((2, 2, 320, 640), jnp.float32),
        in_specs=[pl.BlockSpec(memory_space=pltpu.HBM)],
        out_specs=pl.BlockSpec(memory_space=pltpu.VMEM),
        scratch_shapes=[
            pltpu.VMEM((8 * (32 + PAD), 8, 640), jnp.float32),
            pltpu.VMEM((32 + PAD, TILES, 8, 128), jnp.float32),
            pltpu.VMEM((32 + PAD, TILES, 8, 128), jnp.float32),
            pltpu.VMEM((2, 320, 256), jnp.bfloat16),
            pltpu.VMEM((2, 256, 1280), jnp.bfloat16),
            dma,
            dma((2,)),
            dma((2, 8, 3)),
            dma,
            dma((2, 8)),
            dma((64,)),
            dma((4,)),
        ],
        compiler_params=pltpu.CompilerParams(
            collective_id=0, has_side_effects=True, vmem_limit_bytes=28 * 2**20
        ),
        name="gather_and_multiply",
    )(pltpu.with_memory_space_constraint(shard, pltpu.HBM))
    return sums * (1.0 / 512.0)


def solution(mesh):
    return jax.shard_map(
        per_device,
        mesh=mesh,
        in_specs=(P(None, None, "row", "col"),),
        out_specs=P(None, None, "row", "col"),
        check_vma=False,
    )
```

```python
import jax
import jax.numpy as jnp
from jax import lax
from jax.experimental import pallas as pl
from jax.experimental.pallas import tpu as pltpu
from jax.sharding import PartitionSpec as P

MESH = pl.DeviceIdType.MESH
SEGMENTS = 512
CUT = 3
HALF = 10
PAD = 2
TILES = 2 * HALF


def kernel(x_ref, out_ref, col, row, far, lhs, rhs, own_sem, zs, zr, xs, xr, rr, rs):
    ups, downs, mates, nears = 0, 1, 2, 3
    r = lax.axis_index("row")
    c = lax.axis_index("col")
    z, xl = r // 2, r % 2
    xh, y, core = c // 8, (c // 2) % 4, c % 2
    src_xh, src_y, src_core = z // 8, (z // 2) % 4, z % 2
    dy = (y - src_y + 4) % 4
    home = xh == src_xh
    is_src = home & (dy == 0) & (core == src_core)
    is_src_mate = home & (dy == 0) & (core != src_core)
    is_near = jnp.logical_not(home) & (dy == 0)
    plain = jnp.logical_not(is_src | is_src_mate)
    hops = jnp.where(home, 0, 1) + jnp.where(dy == 0, 0, 1) + jnp.where(dy == 2, 1, 0)
    lag = jnp.where(hops >= 2, 1, 0)
    turns = (hops + 1 + jnp.where(hops == 3, 1, 0), 2 * hops + jnp.where(hops == 3, 0, 1))
    flip = jnp.where(home, 0, 1)

    zdev = [((r + 2) % 32, c), ((r + 30) % 32, c)]
    xdev = (r + 1 - 2 * xl, c)
    mate = (r, c + 1 - 2 * core)

    def ydev(step, k):
        return (r, xh * 8 + ((y + step + 4) % 4) * 2 + k)

    def ndev(k):
        return (r + 1 - 2 * xl, (1 - xh) * 8 + y * 2 + k)

    def blk(s, blocks):
        return pl.ds(8 * (s + PAD) + blocks.start, blocks.stop - blocks.start)

    own = pltpu.make_async_copy(x_ref, col.at[blk(0, slice(0, 8))], own_sem)
    own.start()
    barrier = pltpu.get_barrier_semaphore()
    greet = [zdev[0], zdev[1], xdev, mate]
    greet += [ydev(s, k) for s in (1, -1) for k in (0, 1)] + [ndev(0), ndev(1)]
    for d in greet:
        pl.semaphore_signal(barrier, inc=1, device_id=d, device_id_type=MESH)
    own.wait()
    pl.semaphore_wait(barrier, len(greet))

    A, B = slice(0, CUT), slice(CUT, 8)

    def remote(src, dst, ss, rs, dev):
        return pltpu.make_async_remote_copy(
            src_ref=src, dst_ref=dst, send_sem=ss, recv_sem=rs, device_id=dev, device_id_type=MESH
        )

    def zcopy(t, d, part):
        to = 4 * t - 2 + 2 * d
        fro = jnp.where(t == 1, 0, 4 * t - 6 + 2 * d)
        side, blocks = (1, A) if part == 2 else (0, (B, A)[part])
        return remote(
            col.at[blk(fro + side, blocks)], col.at[blk(to + side, blocks)], zs.at[d], zr.at[d, t - 1, part], zdev[d]
        )

    def last_a():
        return remote(col.at[blk(29, A)], col.at[blk(31, A)], zs.at[1], zr.at[1, 7, 2], zdev[1])

    def last_b():
        return remote(col.at[blk(29, B)], col.at[blk(31, B)], zs.at[1], zr.at[1, 7, 0], zdev[1])

    def xown(part):
        blocks = (A, B)[part]
        return remote(col.at[blk(0, blocks)], col.at[blk(1, blocks)], xs, xr.at[part, 0], xdev)

    def xcopy(t, d):
        slot = 4 * t - 2 + 2 * d
        return remote(col.at[blk(slot, B)], col.at[blk(slot + 1, B)], xs, xr.at[d, t], xdev)

    def half(f):
        return pl.ds(HALF * f, HALF)

    def both(body):
        def one(f, carry):
            body(f)
            return carry

        lax.fori_loop(0, 2, one, 0)

    def rows_copy(s, f, src, way, dev, to=None):
        to = s if to is None else to
        return remote(src.at[s + PAD, half(f)], row.at[to + PAD, half(f)], rs.at[way], rr.at[2 * to + f], dev)

    def rows_wait(s, f):
        ref = row.at[s + PAD, half(f)]
        pltpu.make_async_copy(ref, ref, rr.at[2 * s + f]).wait()

    def sent(shards, way):
        ref = row.at[pl.ds(0, shards)]
        remote(ref, ref, rs.at[way], rr.at[0], mate).wait_send()

    def other(s):
        return s + 1 - 2 * (s % 2)

    def pack(s):
        low = lax.broadcasted_iota(jnp.int32, (32, 128), 1) < 64
        shard = pl.ds(8 * (s + PAD), 8)
        mid = col[shard, :, 256:384].reshape(2, 2, 2, 8, 128)
        re, im = mid[:, 0].reshape(32, 128), mid[:, 1].reshape(32, 128)
        first = jnp.where(low, re, pltpu.roll(im, 64, 1))
        second = jnp.where(low, pltpu.roll(re, 64, 1), im)
        for buf, side in ((row, xl), (far, 1 - xl)):
            packed = jnp.where(side == 0, first, second).reshape(2, 2, 8, 128)
            for f in (0, 1):
                for a in (0, 1):
                    lanes = pl.ds(pl.multiple_of(384 * side + 128 * a, 128), 128)
                    at = HALF * f + 4 * a
                    buf[s + PAD, at : at + 4] = col[pl.ds(8 * (s + PAD) + 4 * f, 4), :, lanes]
                buf[s + PAD, HALF * f + 8 : HALF * f + 10] = packed[f]

    def source_start(s):
        pack(s)
        k = (s // 2) % 2

        @both
        def _(f):
            rows_copy(s, f, far, nears, ndev(k), other(s)).start()
            rows_copy(s, f, row, ups, ydev(1, k)).start()
            rows_copy(s, f, row, downs, ydev(-1, k)).start()
            rows_copy(s, f, row, mates, mate).start()

    def relay_up(kind):
        return is_near | ((dy == 1) & (kind == 0))

    def relay_down(kind):
        return is_near | ((dy == 3) & (kind == 1))

    def relay(s, kind):
        @both
        def _(f):
            rows_wait(s, f)

            @pl.when(relay_up(kind))
            def _():
                rows_copy(s, f, row, ups, ydev(1, core)).start()

            @pl.when(relay_down(kind))
            def _():
                rows_copy(s, f, row, downs, ydev(-1, core)).start()

            rows_copy(s, f, row, mates, mate).start()

    def split(v):
        hi = v.astype(jnp.bfloat16)
        return hi, (v - hi.astype(jnp.float32)).astype(jnp.bfloat16)

    def add(f, n, total, scale=None):
        for side in (0, 1):
            at = 256 * n + 128 * side
            p, j = at // 640, at % 640
            value = out_ref[f, p, :, j : j + 128] + total[:, 128 * side : 128 * side + 128]
            out_ref[f, p, :, j : j + 128] = value if scale is None else value * scale

    def rhs_store(part, at, re, im):
        n = re.shape[0]
        rhs[part, at : at + n, :640], rhs[part, at + n : at + 2 * n, :640] = re, im
        rhs[part, at : at + n, 640:], rhs[part, at + n : at + 2 * n, 640:] = -im, re

    def compute(q, f):
        slots = pl.ds(8 * q, 8)
        for p in (0, 1):
            depth = slice(128 * p, 128 * p + 128)
            for a in (0, 1):
                w = row[slots, pl.ds(HALF * f + 4 * a + 2 * p, 2)].reshape(128, 128).T
                at = pl.ds(pl.multiple_of(64 * xl + 128 * a, 64), 128)
                lhs[0, at, depth], lhs[1, at, depth] = split(w)
        w = row[slots, pl.ds(HALF * f + 8, 2)].reshape(128, 128).T
        at = pl.ds(pl.multiple_of(256 * (1 - xl), 64), 64)
        for part, value in enumerate(split(w)):
            lhs[part, at, :128], lhs[part, at, 128:] = value[:64], value[64:]
        col4 = col.reshape(32 + PAD, 8, 8, 640)
        (re_hi, re_lo), (im_hi, im_lo) = [
            split(col4[slots, pl.ds(4 * f + 2 * p, 2)].reshape(128, 640)) for p in (0, 1)
        ]
        rhs_store(0, 0, re_hi, im_hi)
        rhs_store(1, 0, re_lo, im_lo)
        l_hi, l_lo = lhs[0], lhs[1]
        for n in range(5):
            lanes = slice(256 * n, 256 * n + 256)
            r_hi, r_lo = rhs[0, :, lanes], rhs[1, :, lanes]
            total = jnp.dot(l_hi, r_hi, preferred_element_type=jnp.float32)
            total += jnp.dot(l_lo, r_hi, preferred_element_type=jnp.float32)
            total += jnp.dot(l_hi, r_lo, preferred_element_type=jnp.float32)
            add(f, n, total)

    def compute_last(f):
        slots = slice(30 + PAD, 32 + PAD)

        def stacked(w):
            hi = w.astype(jnp.bfloat16).astype(jnp.float32)
            return jnp.concatenate([hi, w - hi, hi, jnp.zeros_like(w)], axis=0).T.astype(jnp.bfloat16)

        for a in (0, 1):
            w = [row[slots, pl.ds(HALF * f + 4 * a + 2 * p, 2)].reshape(32, 128) for p in (0, 1)]
            lhs[0, pl.ds(pl.multiple_of(64 * xl + 128 * a, 64), 128)] = stacked(jnp.concatenate(w, axis=0))
        w = row[slots, pl.ds(HALF * f + 8, 2)].reshape(32, 128)
        w = stacked(jnp.concatenate([w, pltpu.roll(w, 64, 1)], axis=0))
        lhs[0, pl.ds(pl.multiple_of(256 * (1 - xl), 64), 64)] = w[:64]
        col4 = col.reshape(32 + PAD, 8, 8, 640)
        (re_hi, re_lo), (im_hi, im_lo) = [
            split(col4[slots, pl.ds(4 * f + 2 * p, 2)].reshape(32, 640)) for p in (0, 1)
        ]
        rhs_store(0, 0, re_hi, im_hi)
        rhs_store(0, 64, re_hi, im_hi)
        rhs_store(0, 128, re_lo, im_lo)
        rhs[0, 192:] = jnp.zeros((64, 1280), jnp.bfloat16)
        left = lhs[0]
        for n in range(5):
            total = jnp.dot(left, rhs[0, :, 256 * n : 256 * n + 256], preferred_element_type=jnp.float32)
            add(f, n, total, 1.0 / SEGMENTS)

    for d in (0, 1):
        zcopy(1, d, 0).start()
        zcopy(1, d, 1).start()
    xown(0).start()
    xown(1).start()

    def clear(i, carry):
        out_ref[i // 20, i // 10 % 2, pl.ds(pl.multiple_of(i % 10 * 32, 32), 32)] = jnp.zeros((32, 640), jnp.float32)
        return carry

    def clear_pad(i, carry):
        col[i] = jnp.zeros((8, 640), jnp.float32)
        row[i // 8] = jnp.zeros((TILES, 8, 128), jnp.float32)
        return carry

    lax.fori_loop(0, 40, clear, 0)
    lax.fori_loop(0, 8 * PAD, clear_pad, 0)
    xown(0).wait_recv()
    for d in (0, 1):
        zcopy(1, d, 2).start()

    def source_sends(at, kind):
        @both
        def _(d):
            s = 4 * at - 2 + 2 * d + kind

            @pl.when(is_src & (s >= 0) & (s <= 31))
            def _():
                source_start(s)

    def others_wait(pair, f):
        rows_wait(2 * pair, f)
        rows_wait(2 * pair + 1, f)

    def waited(at):
        q, f = at // 2, at % 2
        for i in (0, 1):
            theirs = 4 * q + 2 * i - 1 + core

            @pl.when(plain & (theirs >= 0))
            def _():
                others_wait(theirs, f)

        @pl.when(is_src_mate)
        def _():
            def wait(pair, carry):
                others_wait(pair, f)
                return carry

            lax.fori_loop(jnp.maximum(4 * q - 1, 0), 4 * q + 3, wait, 0)

        compute(q, f)

    def relays(turn):
        for kind in (1, 0):
            t = turn - turns[kind]
            s = 2 * t - 2 * core + (flip if kind == 0 else 1 - flip)

            @pl.when(plain & (t % 2 == 0) & (s >= 0) & (s <= 31))
            def _():
                relay(s, kind)

    def arrive(k, part):
        for d in (1, 0):
            zcopy(k, d, part).wait_recv()
            if d == 0 and part < 2:
                zcopy(k + 1, d, part).start()
            else:

                @pl.when(k < 7)
                def _():
                    zcopy(k + 1, d, part).start()

            if part == 0:
                xcopy(k, d).start()
            if part == 2 and d == 1:

                @pl.when(k == 7)
                def _():
                    last_a().start()

    def step(k, carry):
        arrive(k, 0)

        @pl.when(k == 1)
        def _():
            xown(1).wait_recv()

        @pl.when(k > 1)
        def _():
            xcopy(k - 1, 1).wait_recv()
            xcopy(k - 1, 0).wait_recv()

        source_sends(k - 1, 1)
        relays(2 * k)
        arrive(k, 1)
        source_sends(k, 0)
        at = k - 3 - lag

        @pl.when(at >= 0)
        def _():
            waited(at)

        arrive(k, 2)
        relays(2 * k + 1)
        return carry

    source_sends(0, 0)
    lax.fori_loop(1, 8, step, 0)
    xcopy(7, 1).wait_recv()
    last_b().start()

    @pl.when(is_src)
    def _():
        xcopy(7, 0).wait_recv()
        source_sends(7, 1)
        zcopy(8, 0, 0).wait_recv()
        zcopy(8, 0, 1).wait_recv()
        source_sends(8, 0)
        last_a().wait_recv()
        last_b().wait_recv()
        source_sends(8, 1)

    def drain(k, carry):
        @pl.when((k == 9) & jnp.logical_not(is_src))
        def _():
            xcopy(7, 0).wait_recv()

        relays(2 * k)
        relays(2 * k + 1)
        at = k - 3 - lag

        @pl.when(at <= 7)
        def _():
            waited(at)

        return carry

    lax.fori_loop(8, 12, drain, 0)

    @pl.when(jnp.logical_not(is_src))
    def _():
        zcopy(8, 0, 0).wait_recv()
        zcopy(8, 0, 1).wait_recv()
        last_a().wait_recv()
        last_b().wait_recv()

    @both
    def _(f):
        @pl.when(is_src_mate | (plain & (core == 0)))
        def _():
            others_wait(15, f)

        compute_last(f)


    for d in (0, 1):
        ref = col.at[pl.ds(0, 7 * (8 + CUT) + 8)]
        remote(ref, ref, zs.at[d], zr.at[0, 0, 0], mate).wait_send()
    ref = col.at[pl.ds(0, 8 + 14 * (8 - CUT))]
    remote(ref, ref, xs, zr.at[0, 0, 0], mate).wait_send()

    @pl.when(is_src)
    def _():
        for way in (ups, downs, mates, nears):
            sent(32, way)

    @pl.when(is_near)
    def _():
        sent(16, ups)
        sent(16, downs)

    @pl.when(dy == 1)
    def _():
        sent(8, ups)

    @pl.when(dy == 3)
    def _():
        sent(8, downs)

    @pl.when(plain)
    def _():
        sent(16, mates)


def store(sums_ref, out_ref, sems):
    copies = [
        pltpu.make_async_copy(sums_ref.at[f, p, h], out_ref.at[f, p, h], sems.at[4 * f + 2 * p + i])
        for f in (0, 1)
        for p in (0, 1)
        for i, h in enumerate((pl.ds(0, 160), pl.ds(160, 160)))
    ]
    for copy in copies:
        copy.start()
    for copy in copies:
        copy.wait()


def per_device(spectra):
    shard = spectra.reshape(8, 8, 640)
    dma = pltpu.SemaphoreType.DMA
    sums = pl.pallas_call(
        kernel,
        out_shape=jax.ShapeDtypeStruct((2, 2, 320, 640), jnp.float32),
        in_specs=[pl.BlockSpec(memory_space=pltpu.HBM)],
        out_specs=pl.BlockSpec(memory_space=pltpu.VMEM),
        scratch_shapes=[
            pltpu.VMEM((8 * (32 + PAD), 8, 640), jnp.float32),
            pltpu.VMEM((32 + PAD, TILES, 8, 128), jnp.float32),
            pltpu.VMEM((32 + PAD, TILES, 8, 128), jnp.float32),
            pltpu.VMEM((2, 320, 256), jnp.bfloat16),
            pltpu.VMEM((2, 256, 1280), jnp.bfloat16),
            dma,
            dma((2,)),
            dma((2, 8, 3)),
            dma,
            dma((2, 8)),
            dma((64,)),
            dma((4,)),
        ],
        compiler_params=pltpu.CompilerParams(
            collective_id=0, has_side_effects=True, vmem_limit_bytes=28 * 2**20
        ),
        name="gather_and_multiply",
    )(pltpu.with_memory_space_constraint(shard, pltpu.HBM))
    return pl.pallas_call(
        store,
        out_shape=jax.ShapeDtypeStruct((2, 2, 320, 640), jnp.float32),
        in_specs=[pl.BlockSpec(memory_space=pl.ANY)],
        out_specs=pl.BlockSpec(memory_space=pl.ANY),
        scratch_shapes=[dma((8,))],
        compiler_params=pltpu.CompilerParams(vmem_limit_bytes=2**20),
        name="store",
    )(sums)


def solution(mesh):
    return jax.shard_map(
        per_device,
        mesh=mesh,
        in_specs=(P(None, None, "row", "col"),),
        out_specs=P(None, None, "row", "col"),
        check_vma=False,
    )
```

```python
import jax
import jax.numpy as jnp
from jax import lax
from jax.experimental import pallas as pl
from jax.experimental.pallas import tpu as pltpu
from jax.sharding import PartitionSpec as P

MESH = pl.DeviceIdType.MESH
SEGMENTS = 512
CUT = 3
HALF = 10
PAD = 2
TILES = 2 * HALF


def kernel(x_ref, out_ref, lhs_last, rhs_last, col, row, far, lhs, rhs, own_sem, zs, zr, xs, xr, rr, rs):
    ups, downs, mates, nears = 0, 1, 2, 3
    r = lax.axis_index("row")
    c = lax.axis_index("col")
    z, xl = r // 2, r % 2
    xh, y, core = c // 8, (c // 2) % 4, c % 2
    src_xh, src_y, src_core = z // 8, (z // 2) % 4, z % 2
    dy = (y - src_y + 4) % 4
    home = xh == src_xh
    is_src = home & (dy == 0) & (core == src_core)
    is_src_mate = home & (dy == 0) & (core != src_core)
    is_near = jnp.logical_not(home) & (dy == 0)
    plain = jnp.logical_not(is_src | is_src_mate)
    hops = jnp.where(home, 0, 1) + jnp.where(dy == 0, 0, 1) + jnp.where(dy == 2, 1, 0)
    lag = jnp.where(hops >= 2, 1, 0)
    turns = (hops + 1 + jnp.where(hops == 3, 1, 0), 2 * hops + jnp.where(hops == 3, 0, 1))
    flip = jnp.where(home, 0, 1)

    zdev = [((r + 2) % 32, c), ((r + 30) % 32, c)]
    xdev = (r + 1 - 2 * xl, c)
    mate = (r, c + 1 - 2 * core)

    def ydev(step, k):
        return (r, xh * 8 + ((y + step + 4) % 4) * 2 + k)

    def ndev(k):
        return (r + 1 - 2 * xl, (1 - xh) * 8 + y * 2 + k)

    def blk(s, blocks):
        return pl.ds(8 * (s + PAD) + blocks.start, blocks.stop - blocks.start)

    own = pltpu.make_async_copy(x_ref, col.at[blk(0, slice(0, 8))], own_sem)
    own.start()
    barrier = pltpu.get_barrier_semaphore()
    greet = [zdev[0], zdev[1], xdev, mate]
    greet += [ydev(s, k) for s in (1, -1) for k in (0, 1)] + [ndev(0), ndev(1)]
    for d in greet:
        pl.semaphore_signal(barrier, inc=1, device_id=d, device_id_type=MESH)
    own.wait()
    pl.semaphore_wait(barrier, len(greet))

    A, B = slice(0, CUT), slice(CUT, 8)

    def remote(src, dst, ss, rs, dev):
        return pltpu.make_async_remote_copy(
            src_ref=src, dst_ref=dst, send_sem=ss, recv_sem=rs, device_id=dev, device_id_type=MESH
        )

    def zcopy(t, d, part):
        to = 4 * t - 2 + 2 * d
        fro = jnp.where(t == 1, 0, 4 * t - 6 + 2 * d)
        side, blocks = (1, A) if part == 2 else (0, (B, A)[part])
        return remote(
            col.at[blk(fro + side, blocks)], col.at[blk(to + side, blocks)], zs.at[d], zr.at[d, t - 1, part], zdev[d]
        )

    def last_a():
        return remote(col.at[blk(29, A)], col.at[blk(31, A)], zs.at[1], zr.at[1, 7, 2], zdev[1])

    def last_b():
        return remote(col.at[blk(29, B)], col.at[blk(31, B)], zs.at[1], zr.at[1, 7, 0], zdev[1])

    def xown(part):
        blocks = (A, B)[part]
        return remote(col.at[blk(0, blocks)], col.at[blk(1, blocks)], xs, xr.at[part, 0], xdev)

    def xcopy(t, d):
        slot = 4 * t - 2 + 2 * d
        return remote(col.at[blk(slot, B)], col.at[blk(slot + 1, B)], xs, xr.at[d, t], xdev)

    def half(f):
        return pl.ds(HALF * f, HALF)

    def both(body):
        def one(f, carry):
            body(f)
            return carry

        lax.fori_loop(0, 2, one, 0)

    def rows_copy(s, f, src, way, dev, to=None):
        to = s if to is None else to
        return remote(src.at[s + PAD, half(f)], row.at[to + PAD, half(f)], rs.at[way], rr.at[2 * to + f], dev)

    def rows_wait(s, f):
        ref = row.at[s + PAD, half(f)]
        pltpu.make_async_copy(ref, ref, rr.at[2 * s + f]).wait()

    def sent(shards, way):
        ref = row.at[pl.ds(0, shards)]
        remote(ref, ref, rs.at[way], rr.at[0], mate).wait_send()

    def other(s):
        return s + 1 - 2 * (s % 2)

    def pack(s):
        low = lax.broadcasted_iota(jnp.int32, (32, 128), 1) < 64
        shard = pl.ds(8 * (s + PAD), 8)
        mid = col[shard, :, 256:384].reshape(2, 2, 2, 8, 128)
        re, im = mid[:, 0].reshape(32, 128), mid[:, 1].reshape(32, 128)
        first = jnp.where(low, re, pltpu.roll(im, 64, 1))
        second = jnp.where(low, pltpu.roll(re, 64, 1), im)
        for buf, side in ((row, xl), (far, 1 - xl)):
            packed = jnp.where(side == 0, first, second).reshape(2, 2, 8, 128)
            for f in (0, 1):
                for a in (0, 1):
                    lanes = pl.ds(pl.multiple_of(384 * side + 128 * a, 128), 128)
                    at = HALF * f + 4 * a
                    buf[s + PAD, at : at + 4] = col[pl.ds(8 * (s + PAD) + 4 * f, 4), :, lanes]
                buf[s + PAD, HALF * f + 8 : HALF * f + 10] = packed[f]

    def source_start(s):
        pack(s)
        k = (s // 2) % 2

        @both
        def _(f):
            rows_copy(s, f, far, nears, ndev(k), other(s)).start()
            rows_copy(s, f, row, ups, ydev(1, k)).start()
            rows_copy(s, f, row, downs, ydev(-1, k)).start()
            rows_copy(s, f, row, mates, mate).start()

    def relay_up(kind):
        return is_near | ((dy == 1) & (core == 1))

    def relay_down(kind):
        return is_near | ((dy == 3) & (core == 0))

    def relay(s, kind):
        @both
        def _(f):
            rows_wait(s, f)

            @pl.when(relay_up(kind))
            def _():
                rows_copy(s, f, row, ups, ydev(1, core)).start()

            @pl.when(relay_down(kind))
            def _():
                rows_copy(s, f, row, downs, ydev(-1, core)).start()

            rows_copy(s, f, row, mates, mate).start()

    def split(v):
        hi = v.astype(jnp.bfloat16)
        return hi, (v - hi.astype(jnp.float32)).astype(jnp.bfloat16)

    def add(f, n, total):
        for side in (0, 1):
            at = 256 * n + 128 * side
            p, j = at // 640, at % 640
            out_ref[f, p, :, j : j + 128] += total[:, 128 * side : 128 * side + 128]

    def rhs_store(ref, at, re, im):
        n = re.shape[0]
        ref[at : at + n, :640], ref[at + n : at + 2 * n, :640] = re, im
        ref[at : at + n, 640:], ref[at + n : at + 2 * n, 640:] = -im, re

    def compute(q, f):
        slots = pl.ds(8 * q, 8)
        for p in (0, 1):
            depth = slice(128 * p, 128 * p + 128)
            for a in (0, 1):
                w = row[slots, pl.ds(HALF * f + 4 * a + 2 * p, 2)].reshape(128, 128).T
                at = pl.ds(pl.multiple_of(64 * xl + 128 * a, 64), 128)
                lhs[0, at, depth], lhs[1, at, depth] = split(w)
        w = row[slots, pl.ds(HALF * f + 8, 2)].reshape(128, 128).T
        at = pl.ds(pl.multiple_of(256 * (1 - xl), 64), 64)
        for part, value in enumerate(split(w)):
            lhs[part, at, :128], lhs[part, at, 128:] = value[:64], value[64:]
        col4 = col.reshape(32 + PAD, 8, 8, 640)
        (re_hi, re_lo), (im_hi, im_lo) = [
            split(col4[slots, pl.ds(4 * f + 2 * p, 2)].reshape(128, 640)) for p in (0, 1)
        ]
        rhs_store(rhs.at[0], 0, re_hi, im_hi)
        rhs_store(rhs.at[1], 0, re_lo, im_lo)
        l_hi, l_lo = lhs[0], lhs[1]
        for n in range(5):
            lanes = slice(256 * n, 256 * n + 256)
            r_hi, r_lo = rhs[0, :, lanes], rhs[1, :, lanes]
            total = jnp.dot(l_hi, r_hi, preferred_element_type=jnp.float32)
            total += jnp.dot(l_lo, r_hi, preferred_element_type=jnp.float32)
            total += jnp.dot(l_hi, r_lo, preferred_element_type=jnp.float32)
            add(f, n, total)

    last = slice(30 + PAD, 32 + PAD)

    def last_columns(f):
        col4 = col.reshape(32 + PAD, 8, 8, 640)
        (re_hi, re_lo), (im_hi, im_lo) = [split(col4[last, pl.ds(4 * f + 2 * p, 2)].reshape(32, 640)) for p in (0, 1)]
        rhs_store(rhs_last.at[f], 0, re_hi, im_hi)
        rhs_store(rhs_last.at[f], 64, re_hi, im_hi)
        rhs_store(rhs_last.at[f], 128, re_lo, im_lo)
        rhs_last[f, 192:] = jnp.zeros((64, 1280), jnp.bfloat16)

    def last_rows(f):
        def stacked(w):
            hi = w.astype(jnp.bfloat16).astype(jnp.float32)
            return jnp.concatenate([hi, w - hi, hi, jnp.zeros_like(w)], axis=0).T.astype(jnp.bfloat16)

        for a in (0, 1):
            w = [row[last, pl.ds(HALF * f + 4 * a + 2 * p, 2)].reshape(32, 128) for p in (0, 1)]
            lhs_last[f, pl.ds(pl.multiple_of(64 * xl + 128 * a, 64), 128)] = stacked(jnp.concatenate(w, axis=0))
        w = row[last, pl.ds(HALF * f + 8, 2)].reshape(32, 128)
        w = stacked(jnp.concatenate([w, pltpu.roll(w, 64, 1)], axis=0))
        lhs_last[f, pl.ds(pl.multiple_of(256 * (1 - xl), 64), 64)] = w[:64]

    for d in (0, 1):
        zcopy(1, d, 0).start()
        zcopy(1, d, 1).start()
    xown(0).start()
    xown(1).start()

    def clear(i, carry):
        out_ref[i // 20, i // 10 % 2, pl.ds(pl.multiple_of(i % 10 * 32, 32), 32)] = jnp.zeros((32, 640), jnp.float32)
        return carry

    def clear_pad(i, carry):
        col[i] = jnp.zeros((8, 640), jnp.float32)
        row[i // 8] = jnp.zeros((TILES, 8, 128), jnp.float32)
        return carry

    lax.fori_loop(0, 40, clear, 0)
    lax.fori_loop(0, 8 * PAD, clear_pad, 0)
    xown(0).wait_recv()
    for d in (0, 1):
        zcopy(1, d, 2).start()

    def source_sends(at, kind):
        @both
        def _(d):
            s = 4 * at - 2 + 2 * d + kind

            @pl.when(is_src & (s >= 0) & (s <= 31))
            def _():
                source_start(s)

    def others_wait(pair, f):
        rows_wait(2 * pair, f)
        rows_wait(2 * pair + 1, f)

    def waited(at):
        q, f = at // 2, at % 2
        for i in (0, 1):
            theirs = 4 * q + 2 * i - 1 + core

            @pl.when(plain & (theirs >= 0))
            def _():
                others_wait(theirs, f)

        @pl.when(is_src_mate)
        def _():
            def wait(pair, carry):
                others_wait(pair, f)
                return carry

            lax.fori_loop(jnp.maximum(4 * q - 1, 0), 4 * q + 3, wait, 0)

        compute(q, f)

    def relays(turn):
        for kind in (1, 0):
            t = turn - turns[kind]
            s = 2 * t - 2 * core + (flip if kind == 0 else 1 - flip)

            @pl.when(plain & (t % 2 == 0) & (s >= 0) & (s <= 31))
            def _():
                relay(s, kind)

    def arrive(k, part):
        for d in (1, 0):
            zcopy(k, d, part).wait_recv()
            if d == 0 and part < 2:
                zcopy(k + 1, d, part).start()
            else:

                @pl.when(k < 7)
                def _():
                    zcopy(k + 1, d, part).start()

            if part == 0:
                xcopy(k, d).start()
            if part == 2 and d == 1:

                @pl.when(k == 7)
                def _():
                    last_a().start()

    def step(k, carry):
        arrive(k, 0)

        @pl.when(k == 1)
        def _():
            xown(1).wait_recv()

        @pl.when(k > 1)
        def _():
            xcopy(k - 1, 1).wait_recv()
            xcopy(k - 1, 0).wait_recv()

        source_sends(k - 1, 1)
        relays(2 * k)
        arrive(k, 1)
        source_sends(k, 0)
        at = k - 3 - lag

        @pl.when(at >= 0)
        def _():
            waited(at)

        arrive(k, 2)
        relays(2 * k + 1)
        return carry

    source_sends(0, 0)
    lax.fori_loop(1, 8, step, 0)
    xcopy(7, 1).wait_recv()
    last_b().start()

    @pl.when(is_src)
    def _():
        xcopy(7, 0).wait_recv()
        source_sends(7, 1)
        zcopy(8, 0, 0).wait_recv()
        zcopy(8, 0, 1).wait_recv()
        source_sends(8, 0)
        last_a().wait_recv()
        last_b().wait_recv()
        source_sends(8, 1)

    def drain(k, carry):
        @pl.when((k == 9) & jnp.logical_not(is_src))
        def _():
            xcopy(7, 0).wait_recv()

        relays(2 * k)
        relays(2 * k + 1)
        at = k - 3 - lag

        @pl.when(at <= 7)
        def _():
            waited(at)

        return carry

    lax.fori_loop(8, 12, drain, 0)

    @pl.when(jnp.logical_not(is_src))
    def _():
        zcopy(8, 0, 0).wait_recv()
        zcopy(8, 0, 1).wait_recv()
        last_a().wait_recv()
        last_b().wait_recv()

    both(last_columns)

    @both
    def _(f):
        @pl.when(is_src_mate | (plain & (core == 0)))
        def _():
            others_wait(15, f)

        last_rows(f)

    for d in (0, 1):
        ref = col.at[pl.ds(0, 7 * (8 + CUT) + 8)]
        remote(ref, ref, zs.at[d], zr.at[0, 0, 0], mate).wait_send()
    ref = col.at[pl.ds(0, 8 + 14 * (8 - CUT))]
    remote(ref, ref, xs, zr.at[0, 0, 0], mate).wait_send()

    @pl.when(is_src)
    def _():
        for way in (ups, downs, mates, nears):
            sent(32, way)

    @pl.when(is_near)
    def _():
        sent(16, ups)
        sent(16, downs)

    @pl.when((dy == 1) & (core == 1))
    def _():
        sent(16, ups)

    @pl.when((dy == 3) & (core == 0))
    def _():
        sent(16, downs)

    @pl.when(plain)
    def _():
        sent(16, mates)


def finish(sums_ref, lhs_ref, rhs_ref, out_ref, buf, sems):
    copies = []
    for f in (0, 1):
        left = lhs_ref[f]
        for n in range(5):
            total = jnp.dot(left, rhs_ref[f, :, 256 * n : 256 * n + 256], preferred_element_type=jnp.float32)
            for side in (0, 1):
                at = 256 * n + 128 * side
                p, j = at // 640, at % 640
                value = sums_ref[f, p, :, j : j + 128] + total[:, 128 * side : 128 * side + 128]
                buf[f, p, :, j : j + 128] = value * (1.0 / SEGMENTS)
                if j == 512:
                    copies.append(pltpu.make_async_copy(buf.at[f, p], out_ref.at[f, p], sems.at[2 * f + p]))
                    copies[-1].start()
    for copy in copies:
        copy.wait()


def per_device(spectra):
    shard = spectra.reshape(8, 8, 640)
    dma = pltpu.SemaphoreType.DMA
    parts = pl.pallas_call(
        kernel,
        out_shape=(
            jax.ShapeDtypeStruct((2, 2, 320, 640), jnp.float32),
            jax.ShapeDtypeStruct((2, 320, 256), jnp.bfloat16),
            jax.ShapeDtypeStruct((2, 256, 1280), jnp.bfloat16),
        ),
        in_specs=[pl.BlockSpec(memory_space=pltpu.HBM)],
        out_specs=(pl.BlockSpec(memory_space=pltpu.VMEM),) * 3,
        scratch_shapes=[
            pltpu.VMEM((8 * (32 + PAD), 8, 640), jnp.float32),
            pltpu.VMEM((32 + PAD, TILES, 8, 128), jnp.float32),
            pltpu.VMEM((32 + PAD, TILES, 8, 128), jnp.float32),
            pltpu.VMEM((2, 320, 256), jnp.bfloat16),
            pltpu.VMEM((2, 256, 1280), jnp.bfloat16),
            dma,
            dma((2,)),
            dma((2, 8, 3)),
            dma,
            dma((2, 8)),
            dma((64,)),
            dma((4,)),
        ],
        compiler_params=pltpu.CompilerParams(
            collective_id=0, has_side_effects=True, vmem_limit_bytes=28 * 2**20
        ),
        name="gather_and_multiply",
    )(pltpu.with_memory_space_constraint(shard, pltpu.HBM))
    return pl.pallas_call(
        finish,
        out_shape=jax.ShapeDtypeStruct((2, 2, 320, 640), jnp.float32),
        in_specs=[pl.BlockSpec(memory_space=pltpu.VMEM)] * 3,
        out_specs=pl.BlockSpec(memory_space=pl.ANY),
        scratch_shapes=[pltpu.VMEM((2, 2, 320, 640), jnp.float32), dma((4,))],
        compiler_params=pltpu.CompilerParams(vmem_limit_bytes=16 * 2**20),
        name="finish",
    )(*parts)


def solution(mesh):
    return jax.shard_map(
        per_device,
        mesh=mesh,
        in_specs=(P(None, None, "row", "col"),),
        out_specs=P(None, None, "row", "col"),
        check_vma=False,
    )
```

```python
import jax
import jax.numpy as jnp
from jax import lax
from jax.experimental import pallas as pl
from jax.experimental.pallas import tpu as pltpu
from jax.sharding import PartitionSpec as P

MESH = pl.DeviceIdType.MESH
SEGMENTS = 512
CUT = 3
HALF = 10
PAD = 2
TILES = 2 * HALF


def kernel(x_ref, out_ref, lhs_last, rhs_last, col, row, far, lhs, rhs, own_sem, zs, zr, xs, xr, rr, rs):
    ups, downs, mates, nears = 0, 1, 2, 3
    r = lax.axis_index("row")
    c = lax.axis_index("col")
    z, xl = r // 2, r % 2
    xh, y, core = c // 8, (c // 2) % 4, c % 2
    src_xh, src_y, src_core = z // 8, (z // 2) % 4, z % 2
    dy = (y - src_y + 4) % 4
    home = xh == src_xh
    is_src = home & (dy == 0) & (core == src_core)
    is_src_mate = home & (dy == 0) & (core != src_core)
    is_near = jnp.logical_not(home) & (dy == 0)
    plain = jnp.logical_not(is_src | is_src_mate)
    hops = jnp.where(home, 0, 1) + jnp.where(dy == 0, 0, 1) + jnp.where(dy == 2, 1, 0)
    lag = jnp.where(hops >= 2, 1, 0)
    turns = (hops + 1 + jnp.where(hops == 3, 1, 0), 2 * hops + jnp.where(hops == 3, 0, 1))
    passes = plain & (core == 1)
    takes = is_src_mate | (plain & (core == 0))
    flip = jnp.where(home, 0, 1)

    zdev = [((r + 2) % 32, c), ((r + 30) % 32, c)]
    xdev = (r + 1 - 2 * xl, c)
    mate = (r, c + 1 - 2 * core)

    def ydev(step, k):
        return (r, xh * 8 + ((y + step + 4) % 4) * 2 + k)

    def ndev(k):
        return (r + 1 - 2 * xl, (1 - xh) * 8 + y * 2 + k)

    def blk(s, blocks):
        return pl.ds(8 * (s + PAD) + blocks.start, blocks.stop - blocks.start)

    own = pltpu.make_async_copy(x_ref, col.at[blk(0, slice(0, 8))], own_sem)
    own.start()
    barrier = pltpu.get_barrier_semaphore()
    greet = [zdev[0], zdev[1], xdev, mate]
    greet += [ydev(s, k) for s in (1, -1) for k in (0, 1)] + [ndev(0), ndev(1)]
    for d in greet:
        pl.semaphore_signal(barrier, inc=1, device_id=d, device_id_type=MESH)
    own.wait()
    pl.semaphore_wait(barrier, len(greet))

    A, B = slice(0, CUT), slice(CUT, 8)

    def remote(src, dst, ss, rs, dev):
        return pltpu.make_async_remote_copy(
            src_ref=src, dst_ref=dst, send_sem=ss, recv_sem=rs, device_id=dev, device_id_type=MESH
        )

    def zcopy(t, d, part):
        to = 4 * t - 2 + 2 * d
        fro = jnp.where(t == 1, 0, 4 * t - 6 + 2 * d)
        side, blocks = (1, A) if part == 2 else (0, (B, A)[part])
        return remote(
            col.at[blk(fro + side, blocks)], col.at[blk(to + side, blocks)], zs.at[d], zr.at[d, t - 1, part], zdev[d]
        )

    def last_a():
        return remote(col.at[blk(29, A)], col.at[blk(31, A)], zs.at[1], zr.at[1, 7, 2], zdev[1])

    def last_b():
        return remote(col.at[blk(29, B)], col.at[blk(31, B)], zs.at[1], zr.at[1, 7, 0], zdev[1])

    def xown(part):
        blocks = (A, B)[part]
        return remote(col.at[blk(0, blocks)], col.at[blk(1, blocks)], xs, xr.at[part, 0], xdev)

    def xcopy(t, d):
        slot = 4 * t - 2 + 2 * d
        return remote(col.at[blk(slot, B)], col.at[blk(slot + 1, B)], xs, xr.at[d, t], xdev)

    def half(f):
        return pl.ds(HALF * f, HALF)

    def both(body):
        def one(f, carry):
            body(f)
            return carry

        lax.fori_loop(0, 2, one, 0)

    def rows_copy(s, f, src, way, dev, to=None):
        to = s if to is None else to
        return remote(src.at[s + PAD, half(f)], row.at[to + PAD, half(f)], rs.at[way], rr.at[2 * to + f], dev)

    def rows_wait(s, f):
        ref = row.at[s + PAD, half(f)]
        pltpu.make_async_copy(ref, ref, rr.at[2 * s + f]).wait()

    def sent(shards, way):
        ref = row.at[pl.ds(0, shards)]
        remote(ref, ref, rs.at[way], rr.at[0], mate).wait_send()

    def other(s):
        return s + 1 - 2 * (s % 2)

    def pack(s):
        low = lax.broadcasted_iota(jnp.int32, (32, 128), 1) < 64
        shard = pl.ds(8 * (s + PAD), 8)
        mid = col[shard, :, 256:384].reshape(2, 2, 2, 8, 128)
        re, im = mid[:, 0].reshape(32, 128), mid[:, 1].reshape(32, 128)
        first = jnp.where(low, re, pltpu.roll(im, 64, 1))
        second = jnp.where(low, pltpu.roll(re, 64, 1), im)
        for buf, side in ((row, xl), (far, 1 - xl)):
            packed = jnp.where(side == 0, first, second).reshape(2, 2, 8, 128)
            for f in (0, 1):
                for a in (0, 1):
                    lanes = pl.ds(pl.multiple_of(384 * side + 128 * a, 128), 128)
                    at = HALF * f + 4 * a
                    buf[s + PAD, at : at + 4] = col[pl.ds(8 * (s + PAD) + 4 * f, 4), :, lanes]
                buf[s + PAD, HALF * f + 8 : HALF * f + 10] = packed[f]

    def source_start(s):
        pack(s)

        @both
        def _(f):
            rows_copy(s, f, far, nears, ndev(1), other(s)).start()
            rows_copy(s, f, row, ups, ydev(1, 1)).start()
            rows_copy(s, f, row, downs, ydev(-1, 1)).start()
            rows_copy(s, f, row, mates, mate).start()

    def relay_up(d):
        return is_near | (dy == 1) if d == 0 else is_near

    def relay_down(d):
        return is_near | (dy == 3) if d == 1 else is_near

    def relay(s, d):
        @both
        def _(f):
            rows_wait(s, f)

            @pl.when(relay_up(d))
            def _():
                rows_copy(s, f, row, ups, ydev(1, 1)).start()

            @pl.when(relay_down(d))
            def _():
                rows_copy(s, f, row, downs, ydev(-1, 1)).start()

            rows_copy(s, f, row, mates, mate).start()

    def split(v):
        hi = v.astype(jnp.bfloat16)
        return hi, (v - hi.astype(jnp.float32)).astype(jnp.bfloat16)

    def add(f, n, total):
        for side in (0, 1):
            at = 256 * n + 128 * side
            p, j = at // 640, at % 640
            out_ref[f, p, :, j : j + 128] += total[:, 128 * side : 128 * side + 128]

    def rhs_store(ref, at, re, im):
        n = re.shape[0]
        ref[at : at + n, :640], ref[at + n : at + 2 * n, :640] = re, im
        ref[at : at + n, 640:], ref[at + n : at + 2 * n, 640:] = -im, re

    def compute(q, f):
        slots = pl.ds(8 * q, 8)
        for p in (0, 1):
            depth = slice(128 * p, 128 * p + 128)
            for a in (0, 1):
                w = row[slots, pl.ds(HALF * f + 4 * a + 2 * p, 2)].reshape(128, 128).T
                at = pl.ds(pl.multiple_of(64 * xl + 128 * a, 64), 128)
                lhs[0, at, depth], lhs[1, at, depth] = split(w)
        w = row[slots, pl.ds(HALF * f + 8, 2)].reshape(128, 128).T
        at = pl.ds(pl.multiple_of(256 * (1 - xl), 64), 64)
        for part, value in enumerate(split(w)):
            lhs[part, at, :128], lhs[part, at, 128:] = value[:64], value[64:]
        col4 = col.reshape(32 + PAD, 8, 8, 640)
        (re_hi, re_lo), (im_hi, im_lo) = [
            split(col4[slots, pl.ds(4 * f + 2 * p, 2)].reshape(128, 640)) for p in (0, 1)
        ]
        rhs_store(rhs.at[0], 0, re_hi, im_hi)
        rhs_store(rhs.at[1], 0, re_lo, im_lo)
        l_hi, l_lo = lhs[0], lhs[1]
        for n in range(5):
            lanes = slice(256 * n, 256 * n + 256)
            r_hi, r_lo = rhs[0, :, lanes], rhs[1, :, lanes]
            total = jnp.dot(l_hi, r_hi, preferred_element_type=jnp.float32)
            total += jnp.dot(l_lo, r_hi, preferred_element_type=jnp.float32)
            total += jnp.dot(l_hi, r_lo, preferred_element_type=jnp.float32)
            add(f, n, total)

    last = slice(30 + PAD, 32 + PAD)

    def last_columns(f):
        col4 = col.reshape(32 + PAD, 8, 8, 640)
        (re_hi, re_lo), (im_hi, im_lo) = [split(col4[last, pl.ds(4 * f + 2 * p, 2)].reshape(32, 640)) for p in (0, 1)]
        rhs_store(rhs_last.at[f], 0, re_hi, im_hi)
        rhs_store(rhs_last.at[f], 64, re_hi, im_hi)
        rhs_store(rhs_last.at[f], 128, re_lo, im_lo)
        rhs_last[f, 192:] = jnp.zeros((64, 1280), jnp.bfloat16)

    def last_rows(f):
        def stacked(w):
            hi = w.astype(jnp.bfloat16).astype(jnp.float32)
            return jnp.concatenate([hi, w - hi, hi, jnp.zeros_like(w)], axis=0).T.astype(jnp.bfloat16)

        for a in (0, 1):
            w = [row[last, pl.ds(HALF * f + 4 * a + 2 * p, 2)].reshape(32, 128) for p in (0, 1)]
            lhs_last[f, pl.ds(pl.multiple_of(64 * xl + 128 * a, 64), 128)] = stacked(jnp.concatenate(w, axis=0))
        w = row[last, pl.ds(HALF * f + 8, 2)].reshape(32, 128)
        w = stacked(jnp.concatenate([w, pltpu.roll(w, 64, 1)], axis=0))
        lhs_last[f, pl.ds(pl.multiple_of(256 * (1 - xl), 64), 64)] = w[:64]

    for d in (0, 1):
        zcopy(1, d, 0).start()
        zcopy(1, d, 1).start()
    xown(0).start()
    xown(1).start()

    def clear(i, carry):
        out_ref[i // 20, i // 10 % 2, pl.ds(pl.multiple_of(i % 10 * 32, 32), 32)] = jnp.zeros((32, 640), jnp.float32)
        return carry

    def clear_pad(i, carry):
        col[i] = jnp.zeros((8, 640), jnp.float32)
        row[i // 8] = jnp.zeros((TILES, 8, 128), jnp.float32)
        return carry

    lax.fori_loop(0, 40, clear, 0)
    lax.fori_loop(0, 8 * PAD, clear_pad, 0)
    xown(0).wait_recv()
    for d in (0, 1):
        zcopy(1, d, 2).start()

    def source_sends(at, kind):
        @both
        def _(d):
            s = 4 * at - 2 + 2 * d + kind

            @pl.when(is_src & (s >= 0) & (s <= 31))
            def _():
                source_start(s)

    def others_wait(pair, f):
        rows_wait(2 * pair, f)
        rows_wait(2 * pair + 1, f)

    def waited(at):
        q, f = at // 2, at % 2

        @pl.when(takes)
        def _():
            def wait(pair, carry):
                others_wait(pair, f)
                return carry

            lax.fori_loop(jnp.maximum(4 * q - 1, 0), 4 * q + 3, wait, 0)

        compute(q, f)

    def relays(turn):
        for kind in (1, 0):
            t = turn - turns[kind]

            @pl.when(passes & (t % 2 == 0))
            def _():
                for d in (0, 1):
                    s = 2 * t - 2 + 2 * d + (flip if kind == 0 else 1 - flip)

                    @pl.when((s >= 0) & (s <= 31))
                    def _():
                        relay(s, d)

    def arrive(k, part):
        for d in (1, 0):
            zcopy(k, d, part).wait_recv()
            if d == 0 and part < 2:
                zcopy(k + 1, d, part).start()
            else:

                @pl.when(k < 7)
                def _():
                    zcopy(k + 1, d, part).start()

            if part == 0:
                xcopy(k, d).start()
            if part == 2 and d == 1:

                @pl.when(k == 7)
                def _():
                    last_a().start()

    def step(k, carry):
        arrive(k, 0)

        @pl.when(k == 1)
        def _():
            xown(1).wait_recv()

        @pl.when(k > 1)
        def _():
            xcopy(k - 1, 1).wait_recv()
            xcopy(k - 1, 0).wait_recv()

        source_sends(k - 1, 1)
        relays(2 * k)
        arrive(k, 1)
        source_sends(k, 0)
        at = k - 3 - lag

        @pl.when(at >= 0)
        def _():
            waited(at)

        arrive(k, 2)
        relays(2 * k + 1)
        return carry

    source_sends(0, 0)
    lax.fori_loop(1, 8, step, 0)
    xcopy(7, 1).wait_recv()
    last_b().start()

    @pl.when(is_src)
    def _():
        xcopy(7, 0).wait_recv()
        source_sends(7, 1)
        zcopy(8, 0, 0).wait_recv()
        zcopy(8, 0, 1).wait_recv()
        source_sends(8, 0)
        last_a().wait_recv()
        last_b().wait_recv()
        source_sends(8, 1)

    def drain(k, carry):
        @pl.when((k == 9) & jnp.logical_not(is_src))
        def _():
            xcopy(7, 0).wait_recv()

        relays(2 * k)
        relays(2 * k + 1)
        at = k - 3 - lag

        @pl.when(at <= 7)
        def _():
            waited(at)

        return carry

    lax.fori_loop(8, 12, drain, 0)

    @pl.when(jnp.logical_not(is_src))
    def _():
        zcopy(8, 0, 0).wait_recv()
        zcopy(8, 0, 1).wait_recv()
        last_a().wait_recv()
        last_b().wait_recv()

    both(last_columns)

    @both
    def _(f):
        @pl.when(takes)
        def _():
            others_wait(15, f)

        last_rows(f)

    for d in (0, 1):
        ref = col.at[pl.ds(0, 7 * (8 + CUT) + 8)]
        remote(ref, ref, zs.at[d], zr.at[0, 0, 0], mate).wait_send()
    ref = col.at[pl.ds(0, 8 + 14 * (8 - CUT))]
    remote(ref, ref, xs, zr.at[0, 0, 0], mate).wait_send()

    @pl.when(is_src)
    def _():
        for way in (ups, downs, mates, nears):
            sent(32, way)

    @pl.when(passes)
    def _():
        sent(32, mates)

    @pl.when(passes & is_near)
    def _():
        sent(32, ups)
        sent(32, downs)

    @pl.when(passes & (dy == 1))
    def _():
        sent(16, ups)

    @pl.when(passes & (dy == 3))
    def _():
        sent(16, downs)


def finish(sums_ref, lhs_ref, rhs_ref, out_ref, buf, sems):
    copies = []
    for f in (0, 1):
        left = lhs_ref[f]
        for n in range(5):
            total = jnp.dot(left, rhs_ref[f, :, 256 * n : 256 * n + 256], preferred_element_type=jnp.float32)
            for side in (0, 1):
                at = 256 * n + 128 * side
                p, j = at // 640, at % 640
                value = sums_ref[f, p, :, j : j + 128] + total[:, 128 * side : 128 * side + 128]
                buf[f, p, :, j : j + 128] = value * (1.0 / SEGMENTS)
                if j == 512:
                    copies.append(pltpu.make_async_copy(buf.at[f, p], out_ref.at[f, p], sems.at[2 * f + p]))
                    copies[-1].start()
    for copy in copies:
        copy.wait()


def per_device(spectra):
    shard = spectra.reshape(8, 8, 640)
    dma = pltpu.SemaphoreType.DMA
    parts = pl.pallas_call(
        kernel,
        out_shape=(
            jax.ShapeDtypeStruct((2, 2, 320, 640), jnp.float32),
            jax.ShapeDtypeStruct((2, 320, 256), jnp.bfloat16),
            jax.ShapeDtypeStruct((2, 256, 1280), jnp.bfloat16),
        ),
        in_specs=[pl.BlockSpec(memory_space=pltpu.HBM)],
        out_specs=(pl.BlockSpec(memory_space=pltpu.VMEM),) * 3,
        scratch_shapes=[
            pltpu.VMEM((8 * (32 + PAD), 8, 640), jnp.float32),
            pltpu.VMEM((32 + PAD, TILES, 8, 128), jnp.float32),
            pltpu.VMEM((32 + PAD, TILES, 8, 128), jnp.float32),
            pltpu.VMEM((2, 320, 256), jnp.bfloat16),
            pltpu.VMEM((2, 256, 1280), jnp.bfloat16),
            dma,
            dma((2,)),
            dma((2, 8, 3)),
            dma,
            dma((2, 8)),
            dma((64,)),
            dma((4,)),
        ],
        compiler_params=pltpu.CompilerParams(
            collective_id=0, has_side_effects=True, vmem_limit_bytes=28 * 2**20
        ),
        name="gather_and_multiply",
    )(pltpu.with_memory_space_constraint(shard, pltpu.HBM))
    return pl.pallas_call(
        finish,
        out_shape=jax.ShapeDtypeStruct((2, 2, 320, 640), jnp.float32),
        in_specs=[pl.BlockSpec(memory_space=pltpu.VMEM)] * 3,
        out_specs=pl.BlockSpec(memory_space=pl.ANY),
        scratch_shapes=[pltpu.VMEM((2, 2, 320, 640), jnp.float32), dma((4,))],
        compiler_params=pltpu.CompilerParams(vmem_limit_bytes=16 * 2**20),
        name="finish",
    )(*parts)


def solution(mesh):
    return jax.shard_map(
        per_device,
        mesh=mesh,
        in_specs=(P(None, None, "row", "col"),),
        out_specs=P(None, None, "row", "col"),
        check_vma=False,
    )
```

```python
import jax
import jax.numpy as jnp
from jax import lax
from jax.experimental import pallas as pl
from jax.experimental.pallas import tpu as pltpu
from jax.sharding import PartitionSpec as P

MESH = pl.DeviceIdType.MESH
SEGMENTS = 512
CUT = 3
HALF = 10
PAD = 2
TILES = 2 * HALF


def kernel(x_ref, out_ref, lhs_last, rhs_last, col, row, far, lhs, rhs, own_sem, zs, zr, xs, xr, rr, rs):
    ups, downs, mates, nears = 0, 1, 2, 3
    r = lax.axis_index("row")
    c = lax.axis_index("col")
    z, xl = r // 2, r % 2
    xh, y, core = c // 8, (c // 2) % 4, c % 2
    src_xh, src_y, src_core = z // 8, (z // 2) % 4, z % 2
    dy = (y - src_y + 4) % 4
    home = xh == src_xh
    is_src = home & (dy == 0) & (core == src_core)
    is_src_mate = home & (dy == 0) & (core != src_core)
    is_near = jnp.logical_not(home) & (dy == 0)
    plain = jnp.logical_not(is_src | is_src_mate)
    hops = jnp.where(home, 0, 1) + jnp.where(dy == 0, 0, 1) + jnp.where(dy == 2, 1, 0)
    lag = jnp.where(hops >= 2, 1, 0)
    turns = (hops + 1 + jnp.where(hops == 3, 1, 0), 2 * hops + jnp.where(hops == 3, 0, 1))
    passes = plain & (core == 1)
    takes = is_src_mate | (plain & (core == 0))
    flip = jnp.where(home, 0, 1)

    zdev = [((r + 2) % 32, c), ((r + 30) % 32, c)]
    xdev = (r + 1 - 2 * xl, c)
    mate = (r, c + 1 - 2 * core)

    def ydev(step, k):
        return (r, xh * 8 + ((y + step + 4) % 4) * 2 + k)

    def ndev(k):
        return (r + 1 - 2 * xl, (1 - xh) * 8 + y * 2 + k)

    def blk(s, blocks):
        return pl.ds(8 * (s + PAD) + blocks.start, blocks.stop - blocks.start)

    own = pltpu.make_async_copy(x_ref, col.at[blk(0, slice(0, 8))], own_sem)
    own.start()
    barrier = pltpu.get_barrier_semaphore()
    for d in [zdev[0], zdev[1], xdev, mate]:
        pl.semaphore_signal(barrier, inc=1, device_id=d, device_id_type=MESH)

    @pl.when(core == 1)
    def _():
        for d in [ydev(s, k) for s in (1, -1) for k in (0, 1)] + [ndev(0), ndev(1)]:
            pl.semaphore_signal(barrier, inc=1, device_id=d, device_id_type=MESH)

    own.wait()
    pl.semaphore_wait(barrier, 7)

    A, B = slice(0, CUT), slice(CUT, 8)

    def remote(src, dst, ss, rs, dev):
        return pltpu.make_async_remote_copy(
            src_ref=src, dst_ref=dst, send_sem=ss, recv_sem=rs, device_id=dev, device_id_type=MESH
        )

    def zcopy(t, d, part):
        to = 4 * t - 2 + 2 * d
        fro = jnp.where(t == 1, 0, 4 * t - 6 + 2 * d)
        side, blocks = (1, A) if part == 2 else (0, (B, A)[part])
        return remote(
            col.at[blk(fro + side, blocks)], col.at[blk(to + side, blocks)], zs.at[d], zr.at[d, t - 1, part], zdev[d]
        )

    def last_a():
        return remote(col.at[blk(29, A)], col.at[blk(31, A)], zs.at[1], zr.at[1, 7, 2], zdev[1])

    def last_b():
        return remote(col.at[blk(29, B)], col.at[blk(31, B)], zs.at[1], zr.at[1, 7, 0], zdev[1])

    def xown(part):
        blocks = (A, B)[part]
        return remote(col.at[blk(0, blocks)], col.at[blk(1, blocks)], xs, xr.at[part, 0], xdev)

    def xcopy(t, d):
        slot = 4 * t - 2 + 2 * d
        return remote(col.at[blk(slot, B)], col.at[blk(slot + 1, B)], xs, xr.at[d, t], xdev)

    def half(f):
        return pl.ds(HALF * f, HALF)

    def both(body):
        def one(f, carry):
            body(f)
            return carry

        lax.fori_loop(0, 2, one, 0)

    def rows_copy(s, f, src, way, dev, to=None):
        to = s if to is None else to
        return remote(src.at[s + PAD, half(f)], row.at[to + PAD, half(f)], rs.at[way], rr.at[2 * to + f], dev)

    def rows_wait(s, f):
        ref = row.at[s + PAD, half(f)]
        pltpu.make_async_copy(ref, ref, rr.at[2 * s + f]).wait()

    def sent(shards, way):
        ref = row.at[pl.ds(0, shards)]
        remote(ref, ref, rs.at[way], rr.at[0], mate).wait_send()

    def other(s):
        return s + 1 - 2 * (s % 2)

    def pack(s):
        low = lax.broadcasted_iota(jnp.int32, (32, 128), 1) < 64
        shard = pl.ds(8 * (s + PAD), 8)
        mid = col[shard, :, 256:384].reshape(2, 2, 2, 8, 128)
        re, im = mid[:, 0].reshape(32, 128), mid[:, 1].reshape(32, 128)
        first = jnp.where(low, re, pltpu.roll(im, 64, 1))
        second = jnp.where(low, pltpu.roll(re, 64, 1), im)
        for buf, side in ((row, xl), (far, 1 - xl)):
            packed = jnp.where(side == 0, first, second).reshape(2, 2, 8, 128)
            for f in (0, 1):
                for a in (0, 1):
                    lanes = pl.ds(pl.multiple_of(384 * side + 128 * a, 128), 128)
                    at = HALF * f + 4 * a
                    buf[s + PAD, at : at + 4] = col[pl.ds(8 * (s + PAD) + 4 * f, 4), :, lanes]
                buf[s + PAD, HALF * f + 8 : HALF * f + 10] = packed[f]

    def source_start(s):
        pack(s)

        @both
        def _(f):
            rows_copy(s, f, far, nears, ndev(1), other(s)).start()
            rows_copy(s, f, row, ups, ydev(1, 1)).start()
            rows_copy(s, f, row, downs, ydev(-1, 1)).start()
            rows_copy(s, f, row, mates, mate).start()

    def relay_up(d):
        return is_near | (dy == 1) if d == 0 else is_near

    def relay_down(d):
        return is_near | (dy == 3) if d == 1 else is_near

    def relay(s, d):
        @both
        def _(f):
            rows_wait(s, f)

            @pl.when(relay_up(d))
            def _():
                rows_copy(s, f, row, ups, ydev(1, 1)).start()

            @pl.when(relay_down(d))
            def _():
                rows_copy(s, f, row, downs, ydev(-1, 1)).start()

            rows_copy(s, f, row, mates, mate).start()

    def split(v):
        hi = v.astype(jnp.bfloat16)
        return hi, (v - hi.astype(jnp.float32)).astype(jnp.bfloat16)

    def add(f, n, total):
        for side in (0, 1):
            at = 256 * n + 128 * side
            p, j = at // 640, at % 640
            out_ref[f, p, :, j : j + 128] += total[:, 128 * side : 128 * side + 128]

    def rhs_store(ref, at, re, im):
        n = re.shape[0]
        ref[at : at + n, :640], ref[at + n : at + 2 * n, :640] = re, im
        ref[at : at + n, 640:], ref[at + n : at + 2 * n, 640:] = -im, re

    def compute(q, f):
        slots = pl.ds(8 * q, 8)
        for p in (0, 1):
            depth = slice(128 * p, 128 * p + 128)
            for a in (0, 1):
                w = row[slots, pl.ds(HALF * f + 4 * a + 2 * p, 2)].reshape(128, 128).T
                at = pl.ds(pl.multiple_of(64 * xl + 128 * a, 64), 128)
                lhs[0, at, depth], lhs[1, at, depth] = split(w)
        w = row[slots, pl.ds(HALF * f + 8, 2)].reshape(128, 128).T
        at = pl.ds(pl.multiple_of(256 * (1 - xl), 64), 64)
        for part, value in enumerate(split(w)):
            lhs[part, at, :128], lhs[part, at, 128:] = value[:64], value[64:]
        col4 = col.reshape(32 + PAD, 8, 8, 640)
        (re_hi, re_lo), (im_hi, im_lo) = [
            split(col4[slots, pl.ds(4 * f + 2 * p, 2)].reshape(128, 640)) for p in (0, 1)
        ]
        rhs_store(rhs.at[0], 0, re_hi, im_hi)
        rhs_store(rhs.at[1], 0, re_lo, im_lo)
        l_hi, l_lo = lhs[0], lhs[1]
        for n in range(5):
            lanes = slice(256 * n, 256 * n + 256)
            r_hi, r_lo = rhs[0, :, lanes], rhs[1, :, lanes]
            total = jnp.dot(l_hi, r_hi, preferred_element_type=jnp.float32)
            total += jnp.dot(l_lo, r_hi, preferred_element_type=jnp.float32)
            total += jnp.dot(l_hi, r_lo, preferred_element_type=jnp.float32)
            add(f, n, total)

    last = slice(30 + PAD, 32 + PAD)

    def last_columns(f):
        col4 = col.reshape(32 + PAD, 8, 8, 640)
        (re_hi, re_lo), (im_hi, im_lo) = [split(col4[last, pl.ds(4 * f + 2 * p, 2)].reshape(32, 640)) for p in (0, 1)]
        rhs_store(rhs_last.at[f], 0, re_hi, im_hi)
        rhs_store(rhs_last.at[f], 64, re_hi, im_hi)
        rhs_store(rhs_last.at[f], 128, re_lo, im_lo)
        rhs_last[f, 192:] = jnp.zeros((64, 1280), jnp.bfloat16)

    def last_rows(f):
        def stacked(w):
            hi = w.astype(jnp.bfloat16).astype(jnp.float32)
            return jnp.concatenate([hi, w - hi, hi, jnp.zeros_like(w)], axis=0).T.astype(jnp.bfloat16)

        for a in (0, 1):
            w = [row[last, pl.ds(HALF * f + 4 * a + 2 * p, 2)].reshape(32, 128) for p in (0, 1)]
            lhs_last[f, pl.ds(pl.multiple_of(64 * xl + 128 * a, 64), 128)] = stacked(jnp.concatenate(w, axis=0))
        w = row[last, pl.ds(HALF * f + 8, 2)].reshape(32, 128)
        w = stacked(jnp.concatenate([w, pltpu.roll(w, 64, 1)], axis=0))
        lhs_last[f, pl.ds(pl.multiple_of(256 * (1 - xl), 64), 64)] = w[:64]

    for d in (0, 1):
        zcopy(1, d, 0).start()
        zcopy(1, d, 1).start()
    xown(0).start()
    xown(1).start()

    def clear(i, carry):
        out_ref[i // 20, i // 10 % 2, pl.ds(pl.multiple_of(i % 10 * 32, 32), 32)] = jnp.zeros((32, 640), jnp.float32)
        return carry

    def clear_pad(i, carry):
        col[i] = jnp.zeros((8, 640), jnp.float32)
        row[i // 8] = jnp.zeros((TILES, 8, 128), jnp.float32)
        return carry

    lax.fori_loop(0, 40, clear, 0)
    lax.fori_loop(0, 8 * PAD, clear_pad, 0)
    xown(0).wait_recv()
    for d in (0, 1):
        zcopy(1, d, 2).start()

    def source_sends(at, kind):
        @both
        def _(d):
            s = 4 * at - 2 + 2 * d + kind

            @pl.when(is_src & (s >= 0) & (s <= 31))
            def _():
                source_start(s)

    def others_wait(pair, f):
        rows_wait(2 * pair, f)
        rows_wait(2 * pair + 1, f)

    def waited(at):
        q, f = at // 2, at % 2

        @pl.when(takes)
        def _():
            def wait(pair, carry):
                others_wait(pair, f)
                return carry

            lax.fori_loop(jnp.maximum(4 * q - 1, 0), 4 * q + 3, wait, 0)

        compute(q, f)

    def relays(turn):
        for kind in (1, 0):
            t = turn - turns[kind]

            @pl.when(passes & (t % 2 == 0))
            def _():
                for d in (0, 1):
                    s = 2 * t - 2 + 2 * d + (flip if kind == 0 else 1 - flip)

                    @pl.when((s >= 0) & (s <= 31))
                    def _():
                        relay(s, d)

    def arrive(k, part):
        for d in (1, 0):
            zcopy(k, d, part).wait_recv()
            if d == 0 and part < 2:
                zcopy(k + 1, d, part).start()
            else:

                @pl.when(k < 7)
                def _():
                    zcopy(k + 1, d, part).start()

            if part == 0:
                xcopy(k, d).start()
            if part == 2 and d == 1:

                @pl.when(k == 7)
                def _():
                    last_a().start()

    def step(k, carry):
        arrive(k, 0)
        relays(2 * k)

        @pl.when(k == 1)
        def _():
            xown(1).wait_recv()

        @pl.when(k > 1)
        def _():
            xcopy(k - 1, 1).wait_recv()
            xcopy(k - 1, 0).wait_recv()

        source_sends(k - 1, 1)
        arrive(k, 1)
        source_sends(k, 0)
        at = k - 3 - lag

        @pl.when(at >= 0)
        def _():
            waited(at)

        arrive(k, 2)
        relays(2 * k + 1)
        return carry

    source_sends(0, 0)
    lax.fori_loop(1, 8, step, 0)
    xcopy(7, 1).wait_recv()
    last_b().start()

    @pl.when(is_src)
    def _():
        xcopy(7, 0).wait_recv()
        source_sends(7, 1)
        zcopy(8, 0, 0).wait_recv()
        zcopy(8, 0, 1).wait_recv()
        source_sends(8, 0)
        last_a().wait_recv()
        last_b().wait_recv()
        source_sends(8, 1)

    def drain(k, carry):
        @pl.when((k == 9) & jnp.logical_not(is_src))
        def _():
            xcopy(7, 0).wait_recv()

        relays(2 * k)
        relays(2 * k + 1)
        at = k - 3 - lag

        @pl.when(at <= 7)
        def _():
            waited(at)

        return carry

    lax.fori_loop(8, 12, drain, 0)

    @pl.when(jnp.logical_not(is_src))
    def _():
        zcopy(8, 0, 0).wait_recv()
        zcopy(8, 0, 1).wait_recv()
        last_a().wait_recv()
        last_b().wait_recv()

    both(last_columns)

    @both
    def _(f):
        @pl.when(takes)
        def _():
            others_wait(15, f)

        last_rows(f)

    for d in (0, 1):
        ref = col.at[pl.ds(0, 7 * (8 + CUT) + 8)]
        remote(ref, ref, zs.at[d], zr.at[0, 0, 0], mate).wait_send()
    ref = col.at[pl.ds(0, 8 + 14 * (8 - CUT))]
    remote(ref, ref, xs, zr.at[0, 0, 0], mate).wait_send()

    @pl.when(is_src)
    def _():
        for way in (ups, downs, mates, nears):
            sent(32, way)

    @pl.when(passes)
    def _():
        sent(32, mates)

    @pl.when(passes & is_near)
    def _():
        sent(32, ups)
        sent(32, downs)

    @pl.when(passes & (dy == 1))
    def _():
        sent(16, ups)

    @pl.when(passes & (dy == 3))
    def _():
        sent(16, downs)


def finish(sums_ref, lhs_ref, rhs_ref, out_ref, buf, sems):
    copies = []
    for f in (0, 1):
        left = lhs_ref[f]
        for n in range(5):
            total = jnp.dot(left, rhs_ref[f, :, 256 * n : 256 * n + 256], preferred_element_type=jnp.float32)
            for side in (0, 1):
                at = 256 * n + 128 * side
                p, j = at // 640, at % 640
                value = sums_ref[f, p, :, j : j + 128] + total[:, 128 * side : 128 * side + 128]
                buf[f, p, :, j : j + 128] = value * (1.0 / SEGMENTS)
                if j == 512:
                    copies.append(pltpu.make_async_copy(buf.at[f, p], out_ref.at[f, p], sems.at[2 * f + p]))
                    copies[-1].start()
    for copy in copies:
        copy.wait()


def per_device(spectra):
    shard = spectra.reshape(8, 8, 640)
    dma = pltpu.SemaphoreType.DMA
    parts = pl.pallas_call(
        kernel,
        out_shape=(
            jax.ShapeDtypeStruct((2, 2, 320, 640), jnp.float32),
            jax.ShapeDtypeStruct((2, 320, 256), jnp.bfloat16),
            jax.ShapeDtypeStruct((2, 256, 1280), jnp.bfloat16),
        ),
        in_specs=[pl.BlockSpec(memory_space=pltpu.HBM)],
        out_specs=(pl.BlockSpec(memory_space=pltpu.VMEM),) * 3,
        scratch_shapes=[
            pltpu.VMEM((8 * (32 + PAD), 8, 640), jnp.float32),
            pltpu.VMEM((32 + PAD, TILES, 8, 128), jnp.float32),
            pltpu.VMEM((32 + PAD, TILES, 8, 128), jnp.float32),
            pltpu.VMEM((2, 320, 256), jnp.bfloat16),
            pltpu.VMEM((2, 256, 1280), jnp.bfloat16),
            dma,
            dma((2,)),
            dma((2, 8, 3)),
            dma,
            dma((2, 8)),
            dma((64,)),
            dma((4,)),
        ],
        compiler_params=pltpu.CompilerParams(
            collective_id=0, has_side_effects=True, vmem_limit_bytes=28 * 2**20
        ),
        name="gather_and_multiply",
    )(pltpu.with_memory_space_constraint(shard, pltpu.HBM))
    return pl.pallas_call(
        finish,
        out_shape=jax.ShapeDtypeStruct((2, 2, 320, 640), jnp.float32),
        in_specs=[pl.BlockSpec(memory_space=pltpu.VMEM)] * 3,
        out_specs=pl.BlockSpec(memory_space=pl.ANY),
        scratch_shapes=[pltpu.VMEM((2, 2, 320, 640), jnp.float32), dma((4,))],
        compiler_params=pltpu.CompilerParams(vmem_limit_bytes=16 * 2**20),
        name="finish",
    )(*parts)


def solution(mesh):
    return jax.shard_map(
        per_device,
        mesh=mesh,
        in_specs=(P(None, None, "row", "col"),),
        out_specs=P(None, None, "row", "col"),
        check_vma=False,
    )
```
